32 devices in a mesh: seq: 8 (over z, y), ch: 4 (over x, core).
Axes of the slice: x: 2, y: 2, z: 4, core: 2. Of those that a mesh axis runs over, the one named last changes fastest.
Arguments:
- attn_query: bfloat16 [1024, 4096], P(('seq', 'ch')), may hold values from -6 to 6
- attn_key: bfloat16 [1024, 4096], P(('seq', 'ch')), may hold values from -6 to 6
- attn_value: bfloat16 [1024, 4096], P(('seq', 'ch')), may hold values from -6 to 6
- attn_output: bfloat16 [1024, 4096], P(('seq', 'ch')), may hold values from -1.796875 to 1.796875
- attn_grad_out: bfloat16 [1024, 4096], P(('seq', 'ch')), may hold values from -6 to 6
- conv_query: bfloat16 [1024, 8192], P(('seq', 'ch')), may hold values from -6 to 6
- conv_key: bfloat16 [1024, 8192], P(('seq', 'ch')), may hold values from -6 to 6
- conv_value: bfloat16 [1024, 8192], P(('seq', 'ch')), may hold values from -6 to 6
- conv_grad_out: bfloat16 [1024, 8192], P(('seq', 'ch')), may hold values from -6 to 6
- conv_filter: bfloat16 [512, 128], P('ch'), may hold values from -0.5 to 0.5
- doc_lengths: int32 [12], replicated, may hold values from 1 to 320, 1024 in all
Outputs:
- grad_attn_query: bfloat16 [1024, 4096], P(('seq', 'ch'))
- grad_attn_key: bfloat16 [1024, 4096], P(('seq', 'ch'))
- grad_attn_value: bfloat16 [1024, 4096], P(('seq', 'ch'))
- grad_conv_query: bfloat16 [1024, 8192], P(('seq', 'ch'))
- grad_conv_key: bfloat16 [1024, 8192], P(('seq', 'ch'))
- grad_conv_value: bfloat16 [1024, 8192], P(('seq', 'ch'))
- grad_filter: float32 [512, 128], P('ch')
The draws below stay inside these ranges and needn't reach their ends.
Inputs may be any that keep to these rules, and one draw needn't show every extreme that they name: `doc_lengths`: the lengths of 12 documents laid end to end in the window; they sum to 1024 and the longest has exactly 320 positions.
All inputs are finite; a program needn't handle non-finite values.
Results may differ from the reference program's by a relative error of at most 0.0049.
Values may be sent and summed in bfloat16 or wider, within the bound.
No kernel may reach another device: no remote copies, remote signals or barrier semaphores. Data moves between devices by JAX's collectives and lax.ppermute only.
A program may use at most 128 MiB of HBM per device.

```python
import math
import jax
import jax.numpy as jnp
import numpy as np
from jax import lax

HEADS = 32
HEAD_DIM = 128
CHANNELS = 8192
GROUP = 16
FILTER_LEN = 128
DOCS = 12
TOKENS = 1024
MOST = 320


def draw_attn_query(key, part):
    base_key = jax.random.fold_in(key, 1)
    values = jnp.clip(jax.random.normal(base_key, (TOKENS, HEADS, HEAD_DIM), jnp.float32), -4.0, 4.0)
    return values.reshape(TOKENS, HEADS * HEAD_DIM).astype(jnp.bfloat16)


def draw_attn_key(key, part):
    base_key = jax.random.fold_in(key, 2)
    values = jnp.clip(jax.random.normal(base_key, (TOKENS, HEADS, HEAD_DIM), jnp.float32), -4.0, 4.0)
    return values.reshape(TOKENS, HEADS * HEAD_DIM).astype(jnp.bfloat16)


def block_levels(key, dims, shards, smallest, top_value):
    def one(dim, parts):
        draws = jax.random.uniform(jax.random.fold_in(jax.random.fold_in(key, 6), dim), (parts,), jnp.float32, smallest / len(shards), top_value / len(shards))
        return jnp.repeat(jnp.exp(draws), dims[dim] // parts).reshape((-1,) + (1,) * (len(dims) - dim - 1))

    gain = one(*shards[0])
    for cut in shards[1:]:
        gain = gain * one(*cut)
    return gain


def length_profile(number_of, total, reach, skew):
    loads = [(1 << 20) // math.isqrt(standing ** skew) + 1 for standing in range(2, number_of + 1)]
    rest, counts = total - reach - (number_of - 1), [1] * (number_of - 1)
    while rest > 0:
        free = [i for i in range(number_of - 1) if counts[i] < reach]
        pool, remaining = sum([loads[i] for i in free]), rest
        for i in free:
            more = min(reach - counts[i], max(1, remaining * loads[i] // pool), rest)
            counts[i] = counts[i] + more
            rest = rest - more
    return np.array([reach] + counts)


def uneven(rng, number_of, total, most, slope):
    if number_of == 2:
        one = jax.random.randint(rng, (), max(1, total - most), min(most, total - 1) + 1)
        return jnp.stack([one, total - one])
    tallies = jnp.asarray(length_profile(number_of, total, most, slope), jnp.int32)
    couples = (number_of - 1) // 2
    giver, receiver = tallies[1:1 + 2 * couples:2], tallies[2:2 + 2 * couples:2]
    slack = jnp.minimum(giver - 1, most - receiver)
    passed = jax.random.randint(jax.random.fold_in(rng, 1), (couples,), 0, 1 << 20) % (slack + 1)
    tallies = tallies.at[1:1 + 2 * couples:2].set(giver - passed).at[2:2 + 2 * couples:2].set(receiver + passed)
    return tallies[jax.random.permutation(jax.random.fold_in(rng, 2), number_of)]


def centred(own_key, shape, deviation, bound, cuts=(), held_as=jnp.bfloat16):
    factor_of = block_levels(own_key, shape, cuts, -0.22, 0.18) if cuts else 1.0
    drawn = jax.random.normal(own_key, shape, jnp.float32) * deviation * factor_of
    return jnp.minimum(jnp.maximum(drawn, -bound), bound).astype(held_as)


def setup_inputs(seed: int = 0) -> dict:
    keys = jax.random.split(jax.random.key(seed), 12)
    attn_query = draw_attn_query(jax.random.fold_in(keys[11], 71), 0)
    attn_key = draw_attn_key(jax.random.fold_in(keys[11], 71), 0)
    attn_value = centred(keys[2], (TOKENS, HEADS * HEAD_DIM), 1.0, 6.0, ((0, 32),))
    attn_output = centred(keys[3], (TOKENS, HEADS * HEAD_DIM), 0.3, 1.796875, ((0, 32),))
    attn_grad_out = centred(keys[4], (TOKENS, HEADS * HEAD_DIM), 1.0, 6.0, ((0, 32),))
    conv_query = centred(keys[5], (TOKENS, CHANNELS), 1.0, 6.0, ((0, 32),))
    conv_key = centred(keys[6], (TOKENS, CHANNELS), 1.0, 6.0, ((0, 32),))
    conv_value = centred(keys[7], (TOKENS, CHANNELS), 1.0, 6.0, ((0, 32),))
    conv_grad_out = centred(keys[8], (TOKENS, CHANNELS), 1.0, 6.0, ((0, 32),))
    conv_filter = centred(keys[9], (CHANNELS // GROUP, FILTER_LEN), FILTER_LEN ** -0.5, 0.5, ((0, 4),))
    doc_lengths = uneven(keys[10], DOCS, TOKENS, MOST, 2).astype(jnp.int32)
    return dict(attn_query=attn_query, attn_key=attn_key, attn_value=attn_value, attn_output=attn_output, attn_grad_out=attn_grad_out, conv_query=conv_query, conv_key=conv_key, conv_value=conv_value, conv_grad_out=conv_grad_out, conv_filter=conv_filter, doc_lengths=doc_lengths)


def doc_index(doc_lengths, positions):
    doc_ends = jnp.cumsum(doc_lengths).astype(jnp.int32)
    return jnp.sum((doc_ends[None, :] <= positions[:, None]).astype(jnp.int32), axis=1)


def reference(attn_query, attn_key, attn_value, attn_output, attn_grad_out, conv_query, conv_key, conv_value, conv_grad_out, conv_filter, doc_lengths):
    scale_factor = 1.0 / (HEAD_DIM ** 0.5)
    positions = jnp.arange(TOKENS, dtype=jnp.int32)
    doc_ids = doc_index(doc_lengths, positions)
    visible = (doc_ids[:, None] == doc_ids[None, :]) & (positions[None, :] <= positions[:, None])

    def per_head(head_slices):
        head_query, head_key, head_value, head_output, head_grad = head_slices
        scores = jnp.dot(head_query, head_key.T, preferred_element_type=jnp.float32) * scale_factor
        row_max = jnp.max(jnp.where(visible, scores, -jnp.inf), axis=1)
        totals = jnp.sum(jnp.where(visible, jnp.exp(scores - row_max[:, None]), 0.0), axis=1)
        log_norm = row_max + jnp.log(totals)
        probs = jnp.where(visible, jnp.exp(scores - log_norm[:, None]), 0.0)
        delta = jnp.sum(head_grad.astype(jnp.float32) * head_output.astype(jnp.float32), axis=1)
        grad_probs = jnp.dot(head_grad, head_value.T, preferred_element_type=jnp.float32)
        grad_scores = probs * (grad_probs - delta[:, None])
        grad_query = jnp.dot(grad_scores, head_key.astype(jnp.float32), precision=lax.Precision.HIGHEST) * scale_factor
        grad_key = jnp.dot(grad_scores.T, head_query.astype(jnp.float32), precision=lax.Precision.HIGHEST) * scale_factor
        grad_value = jnp.dot(probs.T, head_grad.astype(jnp.float32), precision=lax.Precision.HIGHEST)
        return (grad_query, grad_key, grad_value)

    def to_heads(array):
        return array.reshape(TOKENS, HEADS, HEAD_DIM).transpose(1, 0, 2)

    def from_heads(array):
        return array.transpose(1, 0, 2).reshape(TOKENS, HEADS * HEAD_DIM).astype(jnp.bfloat16)

    grad_q_heads, grad_k_heads, grad_v_heads = lax.map(per_head, (to_heads(attn_query), to_heads(attn_key), to_heads(attn_value), to_heads(attn_output), to_heads(attn_grad_out)))

    mixed_rounded = (conv_key.astype(jnp.float32) * conv_value.astype(jnp.float32)).astype(jnp.bfloat16)
    mixed = lax.optimization_barrier(mixed_rounded).astype(jnp.float32)
    out_grad_rounded = (conv_grad_out.astype(jnp.float32) * conv_query.astype(jnp.float32)).astype(jnp.bfloat16)
    out_grad = lax.optimization_barrier(out_grad_rounded).astype(jnp.float32)
    channel_taps = jnp.repeat(conv_filter.astype(jnp.float32), GROUP, axis=0)
    before = jnp.concatenate((jnp.zeros((FILTER_LEN, CHANNELS), jnp.float32), mixed), axis=0)
    after = jnp.concatenate((out_grad, jnp.zeros((FILTER_LEN, CHANNELS), jnp.float32)), axis=0)
    doc_before = jnp.concatenate((jnp.full((FILTER_LEN,), -1, jnp.int32), doc_ids), axis=0)
    doc_after = jnp.concatenate((doc_ids, jnp.full((FILTER_LEN,), -1, jnp.int32)), axis=0)

    def tap_step(tap_index, carried):
        conv_out, mixed_grad, tap_grads = carried
        tap_at = jnp.asarray(tap_index).astype(jnp.int32)
        back_start = (jnp.int32(FILTER_LEN) - tap_at).astype(jnp.int32)
        earlier = lax.dynamic_slice_in_dim(before, back_start, TOKENS, 0)
        earlier_doc = lax.dynamic_slice_in_dim(doc_before, back_start, TOKENS, 0)
        back_valid = (earlier_doc == doc_ids)[:, None]
        tap_row = lax.dynamic_slice_in_dim(channel_taps, tap_at, 1, 1)[:, 0]
        conv_out = conv_out + jnp.where(back_valid, earlier * tap_row[None, :], 0.0)
        tap_sum = jnp.sum(jnp.where(back_valid, out_grad * earlier, 0.0), axis=0)
        tap_grads = lax.dynamic_update_slice_in_dim(tap_grads, tap_sum[None, :], tap_at, 0)
        later = lax.dynamic_slice_in_dim(after, tap_at, TOKENS, 0)
        later_doc = lax.dynamic_slice_in_dim(doc_after, tap_at, TOKENS, 0)
        ahead_valid = (later_doc == doc_ids)[:, None]
        mixed_grad = mixed_grad + jnp.where(ahead_valid, later * tap_row[None, :], 0.0)
        return (conv_out, mixed_grad, tap_grads)

    start_state = (jnp.zeros((TOKENS, CHANNELS), jnp.float32), jnp.zeros((TOKENS, CHANNELS), jnp.float32), jnp.zeros((FILTER_LEN, CHANNELS), jnp.float32))
    conv_out, mixed_grad, tap_grads = lax.fori_loop(0, FILTER_LEN, tap_step, start_state)
    grad_conv_query = (conv_grad_out.astype(jnp.float32) * conv_out).astype(jnp.bfloat16)
    grad_conv_key = (mixed_grad * conv_value.astype(jnp.float32)).astype(jnp.bfloat16)
    grad_conv_value = (mixed_grad * conv_key.astype(jnp.float32)).astype(jnp.bfloat16)
    grad_filter = jnp.sum(tap_grads.reshape(FILTER_LEN, CHANNELS // GROUP, GROUP), axis=2).T
    return (from_heads(grad_q_heads), from_heads(grad_k_heads), from_heads(grad_v_heads), grad_conv_query, grad_conv_key, grad_conv_value, grad_filter)
```

```python
import functools
import math

import jax
import jax.numpy as jnp
from jax import lax
from jax.experimental import pallas as pl
from jax.experimental.pallas import tpu as pltpu
from jax.sharding import PartitionSpec as P

HEAD_DIM = 128
GROUP = 16
FILTER_LEN = 128
LANES = 128
BAND_REACH = 320
DEVICES = ("seq", "ch")
NEG_FILL = -1e30
BF16 = jnp.bfloat16
F32 = jnp.float32

NT = (((1,), (1,)), ((), ()))
NN = (((1,), (0,)), ((), ()))
TN = (((0,), (0,)), ((), ()))


def dot(a, b, dims):
    return lax.dot_general(a, b, dims, preferred_element_type=F32)


def params():
    return pltpu.CompilerParams(vmem_limit_bytes=40 * 1024 * 1024)


def cost(flops, bytes_accessed):
    return pl.CostEstimate(flops=flops, bytes_accessed=bytes_accessed, transcendentals=0)


def doc_start(lens_ref, positions):
    start = jnp.zeros_like(positions)
    end = jnp.int32(0)
    for d in range(lens_ref.shape[0]):
        end = end + lens_ref[d]
        start = jnp.where(positions >= end, end, start)
    return start


def conv_pack_kernel(cq_ref, ck_ref, cv_ref, cg_ref, out_ref):
    rows = cq_ref.shape[0]
    mixed = ck_ref[...].astype(F32) * cv_ref[...].astype(F32)
    grad = cg_ref[...].astype(F32) * cq_ref[...].astype(F32)
    out_ref[0, 0:rows, :] = mixed.astype(BF16)
    out_ref[0, rows:, :] = grad.astype(BF16)


def conv_pack(cq, ck, cv, cg, inner, ch_count):
    rows, channels = cq.shape
    members = inner * ch_count
    width = channels // members
    spec = pl.BlockSpec((rows, width), lambda k: (0, k))
    return pl.pallas_call(
        conv_pack_kernel,
        grid=(members,),
        in_specs=[spec] * 4,
        out_specs=pl.BlockSpec(
            (1, 2 * rows, width), lambda k: (lax.rem(k, inner) * ch_count + k // inner, 0, 0)
        ),
        out_shape=jax.ShapeDtypeStruct((members, 2 * rows, width), BF16),
        compiler_params=params(),
        cost_estimate=cost(4 * rows * channels, 12 * rows * channels),
        name="conv_pack",
    )(cq, ck, cv, cg)


def attn_pack_kernel(rows, q_ref, k_ref, v_ref, o_ref, g_ref, out_ref, prod_ref):
    heads = q_ref.shape[1] // HEAD_DIM
    span = LANES // rows
    offset = lax.rem(lax.axis_index("ch"), span) * rows
    prod_ref[...] = jnp.zeros_like(prod_ref)
    ones = jnp.ones((8, HEAD_DIM), F32)
    row = lax.broadcasted_iota(jnp.int32, (8, LANES), 0)
    for h in range(heads):
        cols = slice(h * HEAD_DIM, (h + 1) * HEAD_DIM)
        out_ref[h, 0:rows, :] = q_ref[:, cols]
        out_ref[h, rows : 2 * rows, :] = k_ref[:, cols]
        out_ref[h, 2 * rows : 3 * rows, :] = v_ref[:, cols]
        out_ref[h, 3 * rows : 4 * rows, :] = g_ref[:, cols]
        prod_ref[pl.ds(pl.multiple_of(offset, rows), rows), :] = g_ref[:, cols].astype(
            F32
        ) * o_ref[:, cols].astype(F32)
        delta = lax.dot_general(
            ones, prod_ref[...], NT, precision=lax.Precision.HIGHEST, preferred_element_type=F32
        )
        high = delta.astype(BF16).astype(F32)
        low = delta - high
        tile = jnp.where(row == 0, high, jnp.where(row == 1, low, 0.0))
        tile = jnp.concatenate([tile, jnp.zeros_like(tile)], axis=0)
        out_ref[h, 4 * rows : 4 * rows + 16, :] = tile.astype(BF16)


def attn_pack(q, k, v, o, g):
    rows, features = q.shape
    heads = features // HEAD_DIM
    step = math.gcd(heads, 8)
    spec = pl.BlockSpec((rows, step * HEAD_DIM), lambda j: (0, j))
    height = 4 * rows + 16
    return pl.pallas_call(
        functools.partial(attn_pack_kernel, rows),
        grid=(heads // step,),
        in_specs=[spec] * 5,
        out_specs=pl.BlockSpec((step, height, HEAD_DIM), lambda j: (j, 0, 0)),
        out_shape=jax.ShapeDtypeStruct((heads, height, HEAD_DIM), BF16),
        scratch_shapes=[pltpu.VMEM((LANES, HEAD_DIM), F32)],
        compiler_params=params(),
        cost_estimate=cost(4 * rows * features, 20 * rows * features),
        name="attn_pack",
    )(q, k, v, o, g)


def split_terms(x):
    high = x.astype(BF16)
    low = (x - high.astype(F32)).astype(BF16)
    return high, low


def attn_kernel(rows, reach, lens_ref, x_ref, out_ref, dk_ref, dv_ref):
    sources = x_ref.shape[0]
    per = LANES // rows
    blocks = sources // per
    scale = 1.0 / math.sqrt(HEAD_DIM)

    def part(first, count, which):
        return x_ref[first * per : (first + count) * per, which * rows : (which + 1) * rows, :].reshape(
            count * LANES, HEAD_DIM
        )

    dk_ref[...] = jnp.zeros_like(dk_ref)
    dv_ref[...] = jnp.zeros_like(dv_ref)
    for i in range(blocks):
        low = max(0, (i * LANES - (reach - 1)) // LANES)
        count = i + 1 - low
        query, grad = part(i, 1, 0), part(i, 1, 3)
        keys, values = part(low, count, 1), part(low, count, 2)
        delta = x_ref[i * per : (i + 1) * per, 4 * rows : 4 * rows + 16, :].astype(F32)
        delta = jnp.sum(jnp.sum(delta, axis=0), axis=0, keepdims=True)
        q_pos = i * LANES + lax.broadcasted_iota(jnp.int32, (8, LANES), 1)
        start = doc_start(lens_ref, q_pos)[0:1]
        k_pos = low * LANES + lax.broadcasted_iota(jnp.int32, (count * LANES, LANES), 0)
        visible = (k_pos >= start) & (k_pos <= q_pos[0:1])
        scores = jnp.where(visible, dot(keys, query, NT) * scale, NEG_FILL)
        top = jnp.max(scores, axis=0, keepdims=True)
        weights = jnp.where(visible, jnp.exp(scores - top), 0.0)
        probs = weights * (1.0 / jnp.sum(weights, axis=0, keepdims=True))
        grad_probs = dot(values, grad, NT)
        grad_scores = probs * (grad_probs - delta)
        span = slice(low * LANES, (i + 1) * LANES)
        p_terms = jnp.concatenate(split_terms(probs), axis=1)
        dv_ref[span, :] += dot(p_terms, jnp.concatenate([grad, grad], axis=0), NN)
        s_high, s_low = split_terms(grad_scores)
        s_terms = jnp.concatenate([s_high, s_low], axis=1)
        dk_ref[span, :] += dot(s_terms, jnp.concatenate([query, query], axis=0), NN)
        dq = dot(s_high, keys, TN) + dot(s_low, keys, TN)
        out_ref[i * per : (i + 1) * per, 0:rows, :] = (
            (dq * scale).astype(BF16).reshape(per, rows, HEAD_DIM)
        )
    for i in range(blocks):
        span = slice(i * LANES, (i + 1) * LANES)
        here = slice(i * per, (i + 1) * per)
        out_ref[here, rows : 2 * rows, :] = (
            (dk_ref[span, :] * scale).astype(BF16).reshape(per, rows, HEAD_DIM)
        )
        out_ref[here, 2 * rows : 3 * rows, :] = (
            dv_ref[span, :].astype(BF16).reshape(per, rows, HEAD_DIM)
        )


def attn_head(lens, x, rows, reach):
    sources = x.shape[0]
    tokens = sources * rows
    return pl.pallas_call(
        functools.partial(attn_kernel, rows, reach),
        in_specs=[
            pl.BlockSpec(memory_space=pltpu.SMEM),
            pl.BlockSpec(memory_space=pltpu.VMEM),
        ],
        out_specs=pl.BlockSpec(memory_space=pltpu.VMEM),
        out_shape=jax.ShapeDtypeStruct((sources, 3 * rows, HEAD_DIM), BF16),
        scratch_shapes=[
            pltpu.VMEM((tokens, HEAD_DIM), F32),
            pltpu.VMEM((tokens, HEAD_DIM), F32),
        ],
        compiler_params=params(),
        cost_estimate=cost(20 * tokens * 512 * HEAD_DIM, 4 * x.size),
        name="attn_head",
    )(lens, x)


def attn_unpack_kernel(rows, x_ref, dq_ref, dk_ref, dv_ref):
    for h in range(x_ref.shape[0]):
        cols = slice(h * HEAD_DIM, (h + 1) * HEAD_DIM)
        dq_ref[:, cols] = x_ref[h, 0:rows, :]
        dk_ref[:, cols] = x_ref[h, rows : 2 * rows, :]
        dv_ref[:, cols] = x_ref[h, 2 * rows : 3 * rows, :]


def attn_unpack(x, rows):
    heads = x.shape[0]
    step = math.gcd(heads, 8)
    spec = pl.BlockSpec((rows, step * HEAD_DIM), lambda j: (0, j))
    shape = jax.ShapeDtypeStruct((rows, heads * HEAD_DIM), BF16)
    return pl.pallas_call(
        functools.partial(attn_unpack_kernel, rows),
        grid=(heads // step,),
        in_specs=[pl.BlockSpec((step, 3 * rows, HEAD_DIM), lambda j: (j, 0, 0))],
        out_specs=[spec] * 3,
        out_shape=[shape] * 3,
        compiler_params=params(),
        cost_estimate=cost(0, 4 * x.size),
        name="attn_unpack",
    )(x)


def conv_kernel(
    rows, inner, ch_count, lens_ref, x_ref, prior_ref, later_ref, tap_ref, rev_ref, out_ref, filt_ref,
    back_ref, front_ref,
):
    sources = x_ref.shape[0]
    per = LANES // rows
    blocks = sources // per
    tile = pl.program_id(0)

    @pl.when(tile == 0)
    def _():
        base = (lax.axis_index("seq") // inner) * (sources * rows)
        shape = (LANES, 2 * LANES)
        down = lax.broadcasted_iota(jnp.int32, shape, 0)
        across = lax.broadcasted_iota(jnp.int32, shape, 1)
        for b in range(blocks):
            out_pos = base + b * LANES + down
            in_pos = base + (b - 1) * LANES + across
            gap = out_pos - in_pos
            near = (gap >= 0) & (gap < FILTER_LEN) & (in_pos >= doc_start(lens_ref, out_pos))
            back_ref[b] = near.astype(F32).astype(BF16)
            in_pos = base + b * LANES + down
            out_pos = base + b * LANES + across
            gap = out_pos - in_pos
            near = (gap >= 0) & (gap < FILTER_LEN) & (in_pos >= doc_start(lens_ref, out_pos))
            front_ref[b] = near.astype(F32).astype(BF16)

    mixed = jnp.concatenate(
        [prior_ref[...].reshape(LANES, LANES), x_ref[:, 0:rows, :].reshape(sources * rows, LANES)],
        axis=0,
    )
    grad = jnp.concatenate(
        [x_ref[:, rows : 2 * rows, :].reshape(sources * rows, LANES), later_ref[...].reshape(LANES, LANES)],
        axis=0,
    )
    lane_group = lax.broadcasted_iota(jnp.int32, (LANES, LANES), 1) // GROUP
    sub = lax.broadcasted_iota(jnp.int32, (8, LANES), 0)
    conv_out = [jnp.zeros((LANES, LANES), F32) for _ in range(blocks)]
    mixed_grad = [jnp.zeros((LANES, LANES), F32) for _ in range(blocks)]
    groups = LANES // GROUP

    def circulant(row):
        rolled = pltpu.roll(jnp.broadcast_to(row, (8, LANES)), 0, 1, stride=1, stride_axis=0)
        pieces = [rolled if a == 0 else pltpu.roll(rolled, 8 * a, 1) for a in range(LANES // 8)]
        full = jnp.concatenate(pieces, axis=0).astype(BF16)
        return jnp.concatenate([full, full], axis=1)

    for g in range(groups):
        mine = lane_group == g
        back_taps = circulant(rev_ref[g : g + 1, :])
        front_taps = circulant(tap_ref[g : g + 1, :])
        outer = jnp.zeros((LANES, LANES), F32)
        for b in range(blocks):
            window = mixed[b * LANES : (b + 2) * LANES]
            ahead = grad[b * LANES : (b + 2) * LANES]
            here = jnp.where(mine, ahead[0:LANES].astype(F32), 0.0).astype(BF16)
            conv_out[b] = jnp.where(mine, dot(back_taps * back_ref[b], window, NN), conv_out[b])
            mixed_grad[b] = jnp.where(mine, dot(front_taps * front_ref[b], ahead, NN), mixed_grad[b])
            full = dot(here, window, NT) * back_ref[b].astype(F32)
            outer = outer + full[:, 0:LANES] + full[:, LANES:]
        folded = outer[0:8]
        for a in range(1, LANES // 8):
            folded = folded + pltpu.roll(outer[8 * a : 8 * a + 8], LANES - 8 * a, 1)
        for bit in (1, 2, 4):
            folded = jnp.where((sub & bit) != 0, pltpu.roll(folded, LANES - bit, 1), folded)
        filt_ref[g : g + 1, :] = jnp.sum(folded, axis=0, keepdims=True)
    for b in range(blocks):
        here = slice(b * per, (b + 1) * per)
        out_ref[here, 0:rows, :] = conv_out[b].astype(BF16).reshape(per, rows, LANES)
        out_ref[here, rows : 2 * rows, :] = mixed_grad[b].astype(BF16).reshape(per, rows, LANES)


def conv_core(lens, x, prior, later, taps, rev_taps, rows, inner, ch_count):
    sources, _, width = x.shape
    per = LANES // rows
    blocks = sources // per
    tiles = width // LANES
    groups = LANES // GROUP
    spec = pl.BlockSpec((sources, 2 * rows, LANES), lambda j: (0, 0, j))
    halo = pl.BlockSpec((per, rows, LANES), lambda j: (0, 0, j))
    tap_spec = pl.BlockSpec((groups, FILTER_LEN), lambda j: (j, 0))
    return pl.pallas_call(
        functools.partial(conv_kernel, rows, inner, ch_count),
        grid=(tiles,),
        in_specs=[pl.BlockSpec(memory_space=pltpu.SMEM), spec, halo, halo, tap_spec, tap_spec],
        out_specs=[spec, tap_spec],
        out_shape=[
            jax.ShapeDtypeStruct(x.shape, BF16),
            jax.ShapeDtypeStruct((width // GROUP, FILTER_LEN), F32),
        ],
        scratch_shapes=[
            pltpu.VMEM((blocks, LANES, 2 * LANES), BF16),
            pltpu.VMEM((blocks, LANES, 2 * LANES), BF16),
        ],
        compiler_params=params(),
        cost_estimate=cost(12 * sources * rows * 2 * LANES * LANES * tiles, 8 * x.size),
        name="conv_core",
    )(lens, x, prior, later, taps, rev_taps)


def conv_unpack_kernel(x_ref, ck_ref, cv_ref, cg_ref, gq_ref, gk_ref, gv_ref):
    rows = ck_ref.shape[0]
    conv_out = x_ref[0, 0:rows, :].astype(F32)
    mixed_grad = x_ref[0, rows : 2 * rows, :].astype(F32)
    gq_ref[...] = (cg_ref[...].astype(F32) * conv_out).astype(BF16)
    gk_ref[...] = (mixed_grad * cv_ref[...].astype(F32)).astype(BF16)
    gv_ref[...] = (mixed_grad * ck_ref[...].astype(F32)).astype(BF16)


def conv_unpack(x, ck, cv, cg, inner, ch_count):
    rows, channels = ck.shape
    members, _, width = x.shape
    spec = pl.BlockSpec((rows, width), lambda k: (0, k))
    shape = jax.ShapeDtypeStruct((rows, channels), BF16)
    return pl.pallas_call(
        conv_unpack_kernel,
        grid=(members,),
        in_specs=[
            pl.BlockSpec(
                (1, 2 * rows, width), lambda k: (lax.rem(k, inner) * ch_count + k // inner, 0, 0)
            ),
            spec,
            spec,
            spec,
        ],
        out_specs=[spec] * 3,
        out_shape=[shape] * 3,
        compiler_params=params(),
        cost_estimate=cost(6 * rows * channels, 16 * rows * channels),
        name="conv_unpack",
    )(x, ck, cv, cg)


def doc_index(doc_lengths, positions):
    doc_ends = jnp.cumsum(doc_lengths)
    return jnp.sum((doc_ends[None, :] <= positions[:, None]).astype(jnp.int32), axis=1)


def split_rows(advance, carried, pieces):
    def one_block(block_index, current):
        sub_parts = tuple(
            lax.dynamic_slice_in_dim(part, block_index * 512, 512, 0) for part in pieces
        )
        return advance(current, sub_parts, block_index * 512)

    return lax.fori_loop(0, pieces[0].shape[0] // 512, one_block, carried)


def attn_gathered(attn_query, attn_key, attn_value, attn_output, attn_grad_out, doc_lengths):
    query_rows, key_rows, value_rows, output_rows, grad_rows = (
        lax.all_to_all(a, "ch", split_axis=1, concat_axis=0, tiled=True)
        for a in (attn_query, attn_key, attn_value, attn_output, attn_grad_out)
    )
    tok_rows = query_rows.shape[0]
    head_count = query_rows.shape[1] // HEAD_DIM
    scale_factor = 1.0 / math.sqrt(HEAD_DIM)
    local_pos = lax.axis_index("seq") * tok_rows + jnp.arange(tok_rows, dtype=jnp.int32)
    local_doc = doc_index(doc_lengths, local_pos)
    query_heads, key_heads, value_heads, output_heads, grad_heads = (
        a.reshape(tok_rows, head_count, HEAD_DIM)
        for a in (query_rows, key_rows, value_rows, output_rows, grad_rows)
    )
    delta_rows = jnp.sum(grad_heads.astype(F32) * output_heads.astype(F32), axis=2)
    delta_heads = delta_rows.T

    def key_step(carried, pieces, key_start):
        key_part, value_part = pieces
        key_pos = key_start + jnp.arange(key_part.shape[0], dtype=jnp.int32)
        key_doc = doc_index(doc_lengths, key_pos)
        visible = (key_doc[None, :] == local_doc[:, None]) & (key_pos[None, :] <= local_pos[:, None])
        running_max, running_sum, running_grad = carried
        scores = (
            jnp.einsum("thd,rhd->htr", query_heads, key_part, preferred_element_type=F32)
            * scale_factor
        )
        new_max = jnp.maximum(
            running_max, jnp.max(jnp.where(visible[None], scores, NEG_FILL), axis=2)
        )
        weights = jnp.where(visible[None], jnp.exp(scores - new_max[:, :, None]), 0.0)
        rescale = jnp.exp(running_max - new_max)
        grad_probs = jnp.einsum(
            "thd,rhd->htr", grad_heads, value_part, preferred_element_type=F32
        )
        weighted = weights * (grad_probs - delta_heads[:, :, None])
        update = jnp.einsum(
            "htr,rhd->htd", weighted, key_part.astype(F32), precision=lax.Precision.HIGHEST
        )
        return (
            new_max,
            running_sum * rescale + jnp.sum(weights, axis=2),
            running_grad * rescale[:, :, None] + update,
        )

    start_state = (
        jnp.full((head_count, tok_rows), NEG_FILL, F32),
        jnp.zeros((head_count, tok_rows), F32),
        jnp.zeros((head_count, tok_rows, HEAD_DIM), F32),
    )
    final_max, final_sum, final_grad = split_rows(
        key_step,
        start_state,
        (
            lax.all_gather(key_heads, "seq", axis=0, tiled=True),
            lax.all_gather(value_heads, "seq", axis=0, tiled=True),
        ),
    )
    lse_rows = (final_max + jnp.log(final_sum)).T
    grad_query = (final_grad * (scale_factor / final_sum)[:, :, None]).transpose(1, 0, 2)
    lse_whole = lax.all_gather(lse_rows, "seq", axis=0, tiled=True)
    delta_whole = lax.all_gather(delta_rows, "seq", axis=0, tiled=True)

    def query_step(carried, pieces, query_start):
        query_part, grad_part = pieces
        part_rows = query_part.shape[0]
        lse_part = lax.dynamic_slice_in_dim(lse_whole, query_start, part_rows, 0)
        delta_part = lax.dynamic_slice_in_dim(delta_whole, query_start, part_rows, 0)
        query_pos = query_start + jnp.arange(part_rows, dtype=jnp.int32)
        query_doc = doc_index(doc_lengths, query_pos)
        visible = (query_doc[:, None] == local_doc[None, :]) & (
            local_pos[None, :] <= query_pos[:, None]
        )
        key_grad, value_grad = carried
        scores = (
            jnp.einsum("rhd,thd->hrt", query_part, key_heads, preferred_element_type=F32)
            * scale_factor
        )
        probs = jnp.where(visible[None], jnp.exp(scores - lse_part.T[:, :, None]), 0.0)
        value_grad = value_grad + jnp.einsum(
            "hrt,rhd->thd", probs, grad_part.astype(F32), precision=lax.Precision.HIGHEST
        )
        grad_probs = jnp.einsum(
            "rhd,thd->hrt", grad_part, value_heads, preferred_element_type=F32
        )
        grad_scores = probs * (grad_probs - delta_part.T[:, :, None])
        key_grad = key_grad + scale_factor * jnp.einsum(
            "hrt,rhd->thd", grad_scores, query_part.astype(F32), precision=lax.Precision.HIGHEST
        )
        return (key_grad, value_grad)

    zero = jnp.zeros((tok_rows, head_count, HEAD_DIM), F32)
    key_grad, value_grad = split_rows(
        query_step,
        (zero, zero),
        (
            lax.all_gather(query_heads, "seq", axis=0, tiled=True),
            lax.all_gather(grad_heads, "seq", axis=0, tiled=True),
        ),
    )
    return tuple(
        lax.all_to_all(
            a.reshape(tok_rows, head_count * HEAD_DIM).astype(BF16),
            "ch",
            split_axis=0,
            concat_axis=1,
            tiled=True,
        )
        for a in (grad_query, key_grad, value_grad)
    )


def shifted(block, distance, count):
    route = [(i, i + distance) for i in range(count) if 0 <= i + distance < count]
    return lax.ppermute(block, DEVICES, route)


def exchanged(block, distance, count):
    return lax.ppermute(block, DEVICES, [(i, i ^ distance) for i in range(count)])


def body(
    attn_query, attn_key, attn_value, attn_output, attn_grad_out,
    conv_query, conv_key, conv_value, conv_grad_out, conv_filter, doc_lengths,
):
    seq_count, ch_count = lax.axis_size("seq"), lax.axis_size("ch")
    count = seq_count * ch_count
    rows, channels = conv_query.shape
    inner = 2
    members = inner * ch_count
    outer = seq_count // inner
    near = [[base + i for i in range(members)] for base in range(0, count, members)]
    heads = attn_query.shape[1] // HEAD_DIM
    head_each = heads == count

    packed = conv_pack(conv_query, conv_key, conv_value, conv_grad_out, inner, ch_count)
    conv_in = lax.all_to_all(
        packed, DEVICES, split_axis=0, concat_axis=0, tiled=True, axis_index_groups=near
    )
    if head_each:
        attn_packed = attn_pack(attn_query, attn_key, attn_value, attn_output, attn_grad_out)
        attn_packed, conv_in = lax.optimization_barrier((attn_packed, conv_in))
        attn_in = lax.all_to_all(attn_packed, DEVICES, split_axis=0, concat_axis=0, tiled=True)

    per = FILTER_LEN // rows
    prior = shifted(conv_in[members - per :, 0:rows, :], members, count)
    later = shifted(conv_in[:per, rows:, :], -members, count)
    group_count = channels // members // GROUP
    y = lax.rem(lax.axis_index("seq"), inner)
    taps = lax.dynamic_slice_in_dim(conv_filter, y * group_count, group_count, 0).astype(F32)
    rev_taps = jnp.roll(taps[:, ::-1], 1, axis=1)
    conv_back, filter_part = conv_core(
        doc_lengths, conv_in, prior, later, taps, rev_taps, rows, inner, ch_count
    )
    if head_each:
        attn_in, conv_back = lax.optimization_barrier((attn_in, conv_back))
    conv_res = lax.all_to_all(
        conv_back, DEVICES, split_axis=0, concat_axis=0, tiled=True, axis_index_groups=near
    )

    distance = members
    while distance < count:
        filter_part = filter_part + exchanged(filter_part, distance, count)
        distance *= 2
    filter_part = jnp.roll(filter_part[:, ::-1], 1, axis=1)
    other = exchanged(filter_part, ch_count, count)
    grad_filter = jnp.where(
        y == 0,
        jnp.concatenate([filter_part, other], axis=0),
        jnp.concatenate([other, filter_part], axis=0),
    )

    if head_each:
        reach = BAND_REACH if rows * count == 1024 else rows * count
        attn_back = attn_head(doc_lengths, attn_in, rows, reach)
        attn_back, conv_res = lax.optimization_barrier((attn_back, conv_res))
        attn_res = lax.all_to_all(attn_back, DEVICES, split_axis=0, concat_axis=0, tiled=True)
    grad_conv = conv_unpack(conv_res, conv_key, conv_value, conv_grad_out, inner, ch_count)
    if head_each:
        grad_attn = attn_unpack(attn_res, rows)
    else:
        grad_attn = attn_gathered(
            attn_query, attn_key, attn_value, attn_output, attn_grad_out, doc_lengths
        )
    return (*grad_attn, *grad_conv, grad_filter)


def solution(mesh):
    rows = P(("seq", "ch"), None)
    return jax.shard_map(
        body,
        mesh=mesh,
        in_specs=(rows,) * 9 + (P("ch", None), P()),
        out_specs=(rows,) * 6 + (P("ch", None),),
        check_vma=False,
    )
```

```python
import functools
import math

import jax
import jax.numpy as jnp
from jax import lax
from jax.experimental import pallas as pl
from jax.experimental.pallas import tpu as pltpu
from jax.sharding import PartitionSpec as P

HEAD_DIM = 128
GROUP = 16
FILTER_LEN = 128
LANES = 128
STEP = 1024
UNROLL = True
BAND_REACH = 320
DEVICES = ("seq", "ch")
NEG_FILL = -1e30
BF16 = jnp.bfloat16
F32 = jnp.float32

NT = (((1,), (1,)), ((), ()))
NN = (((1,), (0,)), ((), ()))
TN = (((0,), (0,)), ((), ()))


def dot(a, b, dims):
    return lax.dot_general(a, b, dims, preferred_element_type=F32)


def params():
    return pltpu.CompilerParams(vmem_limit_bytes=40 * 1024 * 1024)


def cost(flops, bytes_accessed):
    return pl.CostEstimate(flops=flops, bytes_accessed=bytes_accessed, transcendentals=0)


def split_terms(x):
    high = x.astype(BF16)
    low = (x - high.astype(F32)).astype(BF16)
    return high, low


def doc_start(lens_ref, positions):
    start = jnp.zeros_like(positions)
    end = jnp.int32(0)
    for d in range(lens_ref.shape[0]):
        end = end + lens_ref[d]
        start = jnp.where(positions >= end, end, start)
    return start


def member_index(ch_count, inner):
    return lax.rem(lax.axis_index("seq"), inner) * ch_count + lax.axis_index("ch")


def chunk_piece(chunk, ch_count, inner):
    owner = lax.rem(chunk, inner) * ch_count + chunk // inner
    return jnp.bitwise_xor(owner, member_index(ch_count, inner))


def conv_pack_kernel(inner, ch_count, cq_ref, ck_ref, cv_ref, cg_ref, *out_refs):
    rows = cq_ref.shape[0]
    piece = chunk_piece(pl.program_id(0), ch_count, inner)
    mixed = (ck_ref[...].astype(F32) * cv_ref[...].astype(F32)).astype(BF16)
    grad = (cg_ref[...].astype(F32) * cq_ref[...].astype(F32)).astype(BF16)
    for k, out_ref in enumerate(out_refs):

        @pl.when(piece == k)
        def _():
            out_ref[0:rows, :] = mixed
            out_ref[rows:, :] = grad


def conv_pack(cq, ck, cv, cg, inner, ch_count):
    rows, channels = cq.shape
    members = inner * ch_count
    width = channels // members
    spec = pl.BlockSpec((rows, width), lambda k: (0, k))
    return pl.pallas_call(
        functools.partial(conv_pack_kernel, inner, ch_count),
        grid=(members,),
        in_specs=[spec] * 4,
        out_specs=[pl.BlockSpec((2 * rows, width), lambda k: (0, 0))] * members,
        out_shape=[jax.ShapeDtypeStruct((2 * rows, width), BF16)] * members,
        cost_estimate=cost(4 * rows * channels, 12 * rows * channels),
        compiler_params=params(),
        name="conv_pack",
    )(cq, ck, cv, cg)


def conv_join_kernel(rows, inner, ch_count, *refs):
    members = inner * ch_count
    pieces, outs = refs[:members], refs[members:]
    half = members // 2
    me = member_index(ch_count, inner)
    for k, x_ref in enumerate(pieces):
        source = jnp.bitwise_xor(me, k)
        for part in range(2):

            @pl.when(source // half == part)
            def _():
                at = pl.multiple_of((source - part * half) * rows, rows)
                outs[part][pl.ds(at, rows), :] = x_ref[0:rows, :]
                outs[2 + part][pl.ds(at, rows), :] = x_ref[rows : 2 * rows, :]


def conv_join(pieces, rows, inner, ch_count):
    members, width = len(pieces), pieces[0].shape[1]
    step = min(width, 512)
    shape = jax.ShapeDtypeStruct((members * rows // 2, width), BF16)
    return pl.pallas_call(
        functools.partial(conv_join_kernel, rows, inner, ch_count),
        grid=(width // step,),
        in_specs=[pl.BlockSpec((2 * rows, step), lambda j: (0, j))] * members,
        out_specs=[pl.BlockSpec((members * rows // 2, step), lambda j: (0, j))] * 4,
        out_shape=[shape] * 4,
        cost_estimate=cost(0, 8 * members * rows * width),
        name="conv_join",
    )(*pieces)


def attn_pack_kernel(rows, q_ref, k_ref, v_ref, o_ref, g_ref, out_ref):
    heads = q_ref.shape[1] // HEAD_DIM
    span = LANES // rows
    offset = lax.rem(lax.axis_index("ch"), span) * rows
    product = g_ref[...].astype(F32) * o_ref[...].astype(F32)
    shape = (max(heads, 8), heads * HEAD_DIM)
    owner = lax.broadcasted_iota(jnp.int32, shape, 1) // HEAD_DIM
    chosen = (owner == lax.broadcasted_iota(jnp.int32, shape, 0)).astype(F32).astype(BF16)
    high, low = split_terms(product)
    delta = dot(chosen, high, NT) + dot(chosen, low, NT)
    delta = jnp.concatenate([delta, jnp.zeros((delta.shape[0], LANES - rows), F32)], axis=1)
    delta = pltpu.roll(delta, offset, 1)
    high = delta.astype(BF16).astype(F32)
    low = delta - high
    row = lax.broadcasted_iota(jnp.int32, (16, LANES), 0)
    for h in range(heads):
        cols = slice(h * HEAD_DIM, (h + 1) * HEAD_DIM)
        out_ref[h, 0:rows, :] = q_ref[:, cols]
        out_ref[h, rows : 2 * rows, :] = k_ref[:, cols]
        out_ref[h, 2 * rows : 3 * rows, :] = v_ref[:, cols]
        out_ref[h, 3 * rows : 4 * rows, :] = g_ref[:, cols]
        tile = jnp.where(row == 0, high[h : h + 1], jnp.where(row == 1, low[h : h + 1], 0.0))
        out_ref[h, 4 * rows : 4 * rows + 16, :] = tile.astype(BF16)


def attn_pack(q, k, v, o, g):
    rows, features = q.shape
    heads = features // HEAD_DIM
    step = math.gcd(heads, 8)
    spec = pl.BlockSpec((rows, step * HEAD_DIM), lambda j: (0, j))
    height = 4 * rows + 16
    return pl.pallas_call(
        functools.partial(attn_pack_kernel, rows),
        grid=(heads // step,),
        in_specs=[spec] * 5,
        out_specs=pl.BlockSpec((step, height, HEAD_DIM), lambda j: (j, 0, 0)),
        out_shape=jax.ShapeDtypeStruct((heads, height, HEAD_DIM), BF16),
        cost_estimate=cost(4 * rows * features, 20 * rows * features),
        name="attn_pack",
    )(q, k, v, o, g)


def attn_kernel(rows, reach, lens_ref, x_ref, out_ref, dk_ref, dv_ref):
    sources = x_ref.shape[0]
    per = LANES // rows
    blocks = sources // per
    scale = 1.0 / math.sqrt(HEAD_DIM)

    def part(first, count, which):
        return x_ref[first * per : (first + count) * per, which * rows : (which + 1) * rows, :].reshape(
            count * LANES, HEAD_DIM
        )

    dk_ref[...] = jnp.zeros_like(dk_ref)
    dv_ref[...] = jnp.zeros_like(dv_ref)
    for i in range(blocks):
        low = max(0, (i * LANES - (reach - 1)) // LANES)
        count = i + 1 - low
        query, grad = part(i, 1, 0), part(i, 1, 3)
        keys, values = part(low, count, 1), part(low, count, 2)
        delta = x_ref[i * per : (i + 1) * per, 4 * rows : 4 * rows + 16, :].astype(F32)
        delta = jnp.sum(jnp.sum(delta, axis=0), axis=0, keepdims=True)
        q_pos = i * LANES + lax.broadcasted_iota(jnp.int32, (8, LANES), 1)
        start = doc_start(lens_ref, q_pos)[0:1]
        k_pos = low * LANES + lax.broadcasted_iota(jnp.int32, (count * LANES, LANES), 0)
        visible = (k_pos >= start) & (k_pos <= q_pos[0:1])
        scores = jnp.where(visible, dot(keys, query, NT) * scale, NEG_FILL)
        top = jnp.max(scores, axis=0, keepdims=True)
        weights = jnp.where(visible, jnp.exp(scores - top), 0.0)
        probs = weights * (1.0 / jnp.sum(weights, axis=0, keepdims=True))
        grad_probs = dot(values, grad, NT)
        grad_scores = probs * (grad_probs - delta)
        span = slice(low * LANES, (i + 1) * LANES)
        p_terms = jnp.concatenate(split_terms(probs), axis=1)
        dv_ref[span, :] += dot(p_terms, jnp.concatenate([grad, grad], axis=0), NN)
        s_high, s_low = split_terms(grad_scores)
        s_terms = jnp.concatenate([s_high, s_low], axis=1)
        dk_ref[span, :] += dot(s_terms, jnp.concatenate([query, query], axis=0), NN)
        dq = dot(s_high, keys, TN) + dot(s_low, keys, TN)
        out_ref[i * per : (i + 1) * per, 0:rows, :] = (
            (dq * scale).astype(BF16).reshape(per, rows, HEAD_DIM)
        )
    for i in range(blocks):
        span = slice(i * LANES, (i + 1) * LANES)
        here = slice(i * per, (i + 1) * per)
        out_ref[here, rows : 2 * rows, :] = (
            (dk_ref[span, :] * scale).astype(BF16).reshape(per, rows, HEAD_DIM)
        )
        out_ref[here, 2 * rows : 3 * rows, :] = (
            dv_ref[span, :].astype(BF16).reshape(per, rows, HEAD_DIM)
        )


def attn_head(lens, x, rows, reach):
    sources = x.shape[0]
    tokens = sources * rows
    return pl.pallas_call(
        functools.partial(attn_kernel, rows, reach),
        in_specs=[
            pl.BlockSpec(memory_space=pltpu.SMEM),
            pl.BlockSpec(memory_space=pltpu.VMEM),
        ],
        out_specs=pl.BlockSpec(memory_space=pltpu.VMEM),
        out_shape=jax.ShapeDtypeStruct((sources, 3 * rows, HEAD_DIM), BF16),
        scratch_shapes=[
            pltpu.VMEM((tokens, HEAD_DIM), F32),
            pltpu.VMEM((tokens, HEAD_DIM), F32),
        ],
        cost_estimate=cost(20 * tokens * 512 * HEAD_DIM, 4 * x.size),
        name="attn_head",
    )(lens, x)


def attn_unpack_kernel(rows, x_ref, dq_ref, dk_ref, dv_ref):
    for h in range(x_ref.shape[0]):
        cols = slice(h * HEAD_DIM, (h + 1) * HEAD_DIM)
        dq_ref[:, cols] = x_ref[h, 0:rows, :]
        dk_ref[:, cols] = x_ref[h, rows : 2 * rows, :]
        dv_ref[:, cols] = x_ref[h, 2 * rows : 3 * rows, :]


def attn_unpack(x, rows):
    heads = x.shape[0]
    step = math.gcd(heads, 8)
    spec = pl.BlockSpec((rows, step * HEAD_DIM), lambda j: (0, j))
    shape = jax.ShapeDtypeStruct((rows, heads * HEAD_DIM), BF16)
    return pl.pallas_call(
        functools.partial(attn_unpack_kernel, rows),
        grid=(heads // step,),
        in_specs=[pl.BlockSpec((step, 3 * rows, HEAD_DIM), lambda j: (j, 0, 0))],
        out_specs=[spec] * 3,
        out_shape=[shape] * 3,
        cost_estimate=cost(0, 4 * x.size),
        compiler_params=params(),
        name="attn_unpack",
    )(x)


def circulant(row):
    rolled = pltpu.roll(jnp.broadcast_to(row, (8, LANES)), 0, 1, stride=1, stride_axis=0)
    pieces = [rolled if a == 0 else pltpu.roll(rolled, 8 * a, 1) for a in range(LANES // 8)]
    full = jnp.concatenate(pieces, axis=0).astype(BF16)
    return jnp.concatenate([full, full], axis=1)


def unskewed(outer):
    sub = lax.broadcasted_iota(jnp.int32, (8, LANES), 0)
    folded = outer[0:8]
    for a in range(1, LANES // 8):
        folded = folded + pltpu.roll(outer[8 * a : 8 * a + 8], LANES - 8 * a, 1)
    for bit in (1, 2, 4):
        folded = jnp.where((sub & bit) != 0, pltpu.roll(folded, LANES - bit, 1), folded)
    return jnp.sum(folded, axis=0, keepdims=True)


def conv_core_kernel(
    rows, inner, ch_count, lens_ref, tap_ref, rev_ref, prior_ref, m0_ref, m1_ref, g0_ref, g1_ref,
    later_ref, *refs,
):
    members = inner * ch_count
    outs, filt_ref = refs[:members], refs[members]
    back_ref, front_ref, conv_ref, down_ref = refs[members + 1 :]
    me = member_index(ch_count, inner)
    groups = LANES // GROUP
    blocks = 2

    @pl.when(pl.program_id(0) == 0)
    def _():
        base = (lax.axis_index("seq") // inner) * (members * rows)
        shape = (LANES, 2 * LANES)
        down = lax.broadcasted_iota(jnp.int32, shape, 0)
        across = lax.broadcasted_iota(jnp.int32, shape, 1)

        def reached(out_pos, in_pos):
            gap = out_pos - in_pos
            near = (gap >= 0) & (gap < FILTER_LEN) & (in_pos >= doc_start(lens_ref, out_pos))
            return near.astype(F32).astype(BF16)

        for b in range(blocks):
            first = base + b * LANES
            back_ref[b] = reached(first + down, first - LANES + across)
            front_ref[b] = reached(first + across, first + down)

    def one_tile(tile, carried):
        cols = pl.ds(pl.multiple_of(tile * LANES, LANES), LANES)
        mixed = [r[:, cols] for r in (prior_ref, m0_ref, m1_ref)]
        grad = [r[:, cols] for r in (g0_ref, g1_ref, later_ref)]
        lane_group = lax.broadcasted_iota(jnp.int32, (LANES, LANES), 1) // GROUP
        tap_rows = pl.ds(pl.multiple_of(tile * groups, groups), groups)
        taps, rev_taps = tap_ref[tap_rows, :], rev_ref[tap_rows, :]
        back_taps = [circulant(rev_taps[g : g + 1]) for g in range(groups)]
        front_taps = [circulant(taps[g : g + 1]) for g in range(groups)]
        outer = [jnp.zeros((LANES, LANES), F32)] * groups
        for b in range(blocks):
            back, front = back_ref[b], front_ref[b]
            back32 = back.astype(F32)
            window = jnp.concatenate(mixed[b : b + 2], axis=0)
            ahead = jnp.concatenate(grad[b : b + 2], axis=0)
            conv_all = dot(jnp.concatenate([t * back for t in back_taps], axis=0), window, NN)
            down_all = dot(jnp.concatenate([t * front for t in front_taps], axis=0), ahead, NN)
            conv_out = jnp.zeros((LANES, LANES), F32)
            mixed_grad = jnp.zeros((LANES, LANES), F32)
            for g in range(groups):
                mine = lane_group == g
                span = slice(g * LANES, (g + 1) * LANES)
                conv_out = jnp.where(mine, conv_all[span], conv_out)
                mixed_grad = jnp.where(mine, down_all[span], mixed_grad)
                chosen = grad[b] * mine.astype(F32).astype(BF16)
                full = dot(chosen, window, NT) * back32
                outer[g] = outer[g] + full[:, 0:LANES] + full[:, LANES:]
            here = slice(b * LANES, (b + 1) * LANES)
            conv_ref[here, cols] = conv_out.astype(BF16)
            down_ref[here, cols] = mixed_grad.astype(BF16)
        filt_ref[tap_rows, :] = jnp.concatenate([unskewed(o) for o in outer], axis=0)
        return carried

    lax.fori_loop(0, m0_ref.shape[1] // LANES, one_tile, 0, unroll=UNROLL)
    for k, out_ref in enumerate(outs):
        at = pl.multiple_of(jnp.bitwise_xor(me, k) * rows, rows)
        out_ref[0:rows, :] = conv_ref[pl.ds(at, rows), :]
        out_ref[rows : 2 * rows, :] = down_ref[pl.ds(at, rows), :]


def conv_core(lens, taps, rev_taps, arrays, rows, inner, ch_count):
    members = inner * ch_count
    width = arrays[0].shape[1]
    step = min(width, STEP)
    spec = pl.BlockSpec((LANES, step), lambda j: (0, j))
    piece = pl.BlockSpec((2 * rows, step), lambda j: (0, j))
    tap_spec = pl.BlockSpec((step // GROUP, FILTER_LEN), lambda j: (j, 0))
    return pl.pallas_call(
        functools.partial(conv_core_kernel, rows, inner, ch_count),
        grid=(width // step,),
        in_specs=[pl.BlockSpec(memory_space=pltpu.SMEM), tap_spec, tap_spec] + [spec] * 6,
        out_specs=[piece] * members + [tap_spec],
        out_shape=[jax.ShapeDtypeStruct((2 * rows, width), BF16)] * members
        + [jax.ShapeDtypeStruct((width // GROUP, FILTER_LEN), F32)],
        scratch_shapes=[pltpu.VMEM((2, LANES, 2 * LANES), BF16)] * 2
        + [pltpu.VMEM((2 * LANES, step), BF16)] * 2,
        cost_estimate=cost(96 * LANES * LANES * width, 24 * LANES * width),
        name="conv_core",
    )(lens, taps, rev_taps, *arrays)


def conv_unpack_kernel(inner, ch_count, ck_ref, cv_ref, cg_ref, *refs):
    members = inner * ch_count
    pieces, (gq_ref, gk_ref, gv_ref) = refs[:members], refs[members:]
    rows = ck_ref.shape[0]
    piece = chunk_piece(pl.program_id(0), ch_count, inner)
    for k, x_ref in enumerate(pieces):

        @pl.when(piece == k)
        def _():
            conv_out = x_ref[0:rows, :].astype(F32)
            mixed_grad = x_ref[rows : 2 * rows, :].astype(F32)
            gq_ref[...] = (cg_ref[...].astype(F32) * conv_out).astype(BF16)
            gk_ref[...] = (mixed_grad * cv_ref[...].astype(F32)).astype(BF16)
            gv_ref[...] = (mixed_grad * ck_ref[...].astype(F32)).astype(BF16)


def conv_unpack(pieces, ck, cv, cg, inner, ch_count):
    rows, channels = ck.shape
    members = inner * ch_count
    width = channels // members
    spec = pl.BlockSpec((rows, width), lambda k: (0, k))
    shape = jax.ShapeDtypeStruct((rows, channels), BF16)
    return pl.pallas_call(
        functools.partial(conv_unpack_kernel, inner, ch_count),
        grid=(members,),
        in_specs=[spec] * 3 + [pl.BlockSpec((2 * rows, width), lambda k: (0, 0))] * members,
        out_specs=[spec] * 3,
        out_shape=[shape] * 3,
        cost_estimate=cost(6 * rows * channels, 16 * rows * channels),
        compiler_params=params(),
        name="conv_unpack",
    )(ck, cv, cg, *pieces)


def doc_index(doc_lengths, positions):
    doc_ends = jnp.cumsum(doc_lengths)
    return jnp.sum((doc_ends[None, :] <= positions[:, None]).astype(jnp.int32), axis=1)


def split_rows(advance, carried, pieces):
    def one_block(block_index, current):
        sub_parts = tuple(
            lax.dynamic_slice_in_dim(part, block_index * 512, 512, 0) for part in pieces
        )
        return advance(current, sub_parts, block_index * 512)

    return lax.fori_loop(0, pieces[0].shape[0] // 512, one_block, carried)


def attn_gathered(attn_query, attn_key, attn_value, attn_output, attn_grad_out, doc_lengths):
    query_rows, key_rows, value_rows, output_rows, grad_rows = (
        lax.all_to_all(a, "ch", split_axis=1, concat_axis=0, tiled=True)
        for a in (attn_query, attn_key, attn_value, attn_output, attn_grad_out)
    )
    tok_rows = query_rows.shape[0]
    head_count = query_rows.shape[1] // HEAD_DIM
    scale_factor = 1.0 / math.sqrt(HEAD_DIM)
    local_pos = lax.axis_index("seq") * tok_rows + jnp.arange(tok_rows, dtype=jnp.int32)
    local_doc = doc_index(doc_lengths, local_pos)
    query_heads, key_heads, value_heads, output_heads, grad_heads = (
        a.reshape(tok_rows, head_count, HEAD_DIM)
        for a in (query_rows, key_rows, value_rows, output_rows, grad_rows)
    )
    delta_rows = jnp.sum(grad_heads.astype(F32) * output_heads.astype(F32), axis=2)
    delta_heads = delta_rows.T

    def key_step(carried, pieces, key_start):
        key_part, value_part = pieces
        key_pos = key_start + jnp.arange(key_part.shape[0], dtype=jnp.int32)
        key_doc = doc_index(doc_lengths, key_pos)
        visible = (key_doc[None, :] == local_doc[:, None]) & (key_pos[None, :] <= local_pos[:, None])
        running_max, running_sum, running_grad = carried
        scores = (
            jnp.einsum("thd,rhd->htr", query_heads, key_part, preferred_element_type=F32)
            * scale_factor
        )
        new_max = jnp.maximum(
            running_max, jnp.max(jnp.where(visible[None], scores, NEG_FILL), axis=2)
        )
        weights = jnp.where(visible[None], jnp.exp(scores - new_max[:, :, None]), 0.0)
        rescale = jnp.exp(running_max - new_max)
        grad_probs = jnp.einsum(
            "thd,rhd->htr", grad_heads, value_part, preferred_element_type=F32
        )
        weighted = weights * (grad_probs - delta_heads[:, :, None])
        update = jnp.einsum(
            "htr,rhd->htd", weighted, key_part.astype(F32), precision=lax.Precision.HIGHEST
        )
        return (
            new_max,
            running_sum * rescale + jnp.sum(weights, axis=2),
            running_grad * rescale[:, :, None] + update,
        )

    start_state = (
        jnp.full((head_count, tok_rows), NEG_FILL, F32),
        jnp.zeros((head_count, tok_rows), F32),
        jnp.zeros((head_count, tok_rows, HEAD_DIM), F32),
    )
    final_max, final_sum, final_grad = split_rows(
        key_step,
        start_state,
        (
            lax.all_gather(key_heads, "seq", axis=0, tiled=True),
            lax.all_gather(value_heads, "seq", axis=0, tiled=True),
        ),
    )
    lse_rows = (final_max + jnp.log(final_sum)).T
    grad_query = (final_grad * (scale_factor / final_sum)[:, :, None]).transpose(1, 0, 2)
    lse_whole = lax.all_gather(lse_rows, "seq", axis=0, tiled=True)
    delta_whole = lax.all_gather(delta_rows, "seq", axis=0, tiled=True)

    def query_step(carried, pieces, query_start):
        query_part, grad_part = pieces
        part_rows = query_part.shape[0]
        lse_part = lax.dynamic_slice_in_dim(lse_whole, query_start, part_rows, 0)
        delta_part = lax.dynamic_slice_in_dim(delta_whole, query_start, part_rows, 0)
        query_pos = query_start + jnp.arange(part_rows, dtype=jnp.int32)
        query_doc = doc_index(doc_lengths, query_pos)
        visible = (query_doc[:, None] == local_doc[None, :]) & (
            local_pos[None, :] <= query_pos[:, None]
        )
        key_grad, value_grad = carried
        scores = (
            jnp.einsum("rhd,thd->hrt", query_part, key_heads, preferred_element_type=F32)
            * scale_factor
        )
        probs = jnp.where(visible[None], jnp.exp(scores - lse_part.T[:, :, None]), 0.0)
        value_grad = value_grad + jnp.einsum(
            "hrt,rhd->thd", probs, grad_part.astype(F32), precision=lax.Precision.HIGHEST
        )
        grad_probs = jnp.einsum(
            "rhd,thd->hrt", grad_part, value_heads, preferred_element_type=F32
        )
        grad_scores = probs * (grad_probs - delta_part.T[:, :, None])
        key_grad = key_grad + scale_factor * jnp.einsum(
            "hrt,rhd->thd", grad_scores, query_part.astype(F32), precision=lax.Precision.HIGHEST
        )
        return (key_grad, value_grad)

    zero = jnp.zeros((tok_rows, head_count, HEAD_DIM), F32)
    key_grad, value_grad = split_rows(
        query_step,
        (zero, zero),
        (
            lax.all_gather(query_heads, "seq", axis=0, tiled=True),
            lax.all_gather(grad_heads, "seq", axis=0, tiled=True),
        ),
    )
    return tuple(
        lax.all_to_all(
            a.reshape(tok_rows, head_count * HEAD_DIM).astype(BF16),
            "ch",
            split_axis=0,
            concat_axis=1,
            tiled=True,
        )
        for a in (grad_query, key_grad, value_grad)
    )


def shifted(block, distance, count):
    route = [(i, i + distance) for i in range(count) if 0 <= i + distance < count]
    return lax.ppermute(block, DEVICES, route)


def exchanged(block, distance, count):
    return lax.ppermute(block, DEVICES, [(i, i ^ distance) for i in range(count)])


def body(
    attn_query, attn_key, attn_value, attn_output, attn_grad_out,
    conv_query, conv_key, conv_value, conv_grad_out, conv_filter, doc_lengths,
):
    seq_count, ch_count = lax.axis_size("seq"), lax.axis_size("ch")
    count = seq_count * ch_count
    rows, channels = conv_query.shape
    inner = 2
    members = inner * ch_count
    outer = seq_count // inner
    heads = attn_query.shape[1] // HEAD_DIM
    head_each = heads == count

    reach = BAND_REACH if rows * count == 1024 else rows * count

    if head_each:
        attn_packed = attn_pack(attn_query, attn_key, attn_value, attn_output, attn_grad_out)
        attn_in = lax.all_to_all(attn_packed, DEVICES, split_axis=0, concat_axis=0, tiled=True)

    packed = conv_pack(conv_query, conv_key, conv_value, conv_grad_out, inner, ch_count)
    pieces = [packed[0]] + [exchanged(packed[k], k, count) for k in range(1, members)]
    mixed_lo, mixed_hi, grad_lo, grad_hi = conv_join(pieces, rows, inner, ch_count)
    if head_each:
        attn_in, mixed_hi, grad_lo = lax.optimization_barrier((attn_in, mixed_hi, grad_lo))
    prior, later = shifted(mixed_hi, members, count), shifted(grad_lo, -members, count)
    group_count = channels // members // GROUP
    y = lax.rem(lax.axis_index("seq"), inner)
    taps = lax.dynamic_slice_in_dim(conv_filter, y * group_count, group_count, 0).astype(F32)
    rev_taps = jnp.roll(taps[:, ::-1], 1, axis=1)
    if head_each:
        attn_back = attn_head(doc_lengths, attn_in, rows, reach)
        attn_back, prior, later = lax.optimization_barrier((attn_back, prior, later))
        attn_res = lax.all_to_all(attn_back, DEVICES, split_axis=0, concat_axis=0, tiled=True)
    own = (prior, mixed_lo, mixed_hi, grad_lo, grad_hi, later)
    *conv_back, filter_part = conv_core(
        doc_lengths, taps, rev_taps, own, rows, inner, ch_count
    )
    conv_res = [conv_back[0]] + [exchanged(conv_back[k], k, count) for k in range(1, members)]

    filter_part, conv_res[2] = lax.optimization_barrier((filter_part, conv_res[2]))
    distance = members
    while distance < count:
        filter_part = filter_part + exchanged(filter_part, distance, count)
        distance *= 2
    filter_part = jnp.roll(filter_part[:, ::-1], 1, axis=1)
    other = exchanged(filter_part, ch_count, count)
    grad_filter = jnp.where(
        y == 0,
        jnp.concatenate([filter_part, other], axis=0),
        jnp.concatenate([other, filter_part], axis=0),
    )
    if head_each:
        grad_attn = attn_unpack(attn_res, rows)
        *grad_attn, conv_res[-1] = lax.optimization_barrier((*grad_attn, conv_res[-1]))
    else:
        grad_attn = attn_gathered(
            attn_query, attn_key, attn_value, attn_output, attn_grad_out, doc_lengths
        )
    grad_conv = conv_unpack(conv_res, conv_key, conv_value, conv_grad_out, inner, ch_count)
    return (*grad_attn, *grad_conv, grad_filter)


def solution(mesh):
    rows = P(("seq", "ch"), None)
    return jax.shard_map(
        body,
        mesh=mesh,
        in_specs=(rows,) * 9 + (P("ch", None), P()),
        out_specs=(rows,) * 6 + (P("ch", None),),
        check_vma=False,
    )
```

```python
import functools
import math

import jax
import jax.numpy as jnp
from jax import lax
from jax.experimental import pallas as pl
from jax.experimental.pallas import tpu as pltpu
from jax.sharding import PartitionSpec as P

HEAD_DIM = 128
GROUP = 16
FILTER_LEN = 128
LANES = 128
EACH = 2
BAND_REACH = 320
DEVICES = ("seq", "ch")
NEG_FILL = -1e30
BF16 = jnp.bfloat16
F32 = jnp.float32

NT = (((1,), (1,)), ((), ()))
NN = (((1,), (0,)), ((), ()))
TN = (((0,), (0,)), ((), ()))


def dot(a, b, dims):
    return lax.dot_general(a, b, dims, preferred_element_type=F32)


def params():
    return pltpu.CompilerParams(vmem_limit_bytes=40 * 1024 * 1024)


def cost(flops, bytes_accessed):
    return pl.CostEstimate(flops=flops, bytes_accessed=bytes_accessed, transcendentals=0)


def split_terms(x):
    high = x.astype(BF16)
    low = (x - high.astype(F32)).astype(BF16)
    return high, low


def doc_start(lens_ref, positions):
    start = jnp.zeros_like(positions)
    end = jnp.int32(0)
    for d in range(lens_ref.shape[0]):
        end = end + lens_ref[d]
        start = jnp.where(positions >= end, end, start)
    return start


def member_index(ch_count, inner):
    return lax.rem(lax.axis_index("seq"), inner) * ch_count + lax.axis_index("ch")


def chunk_piece(chunk, ch_count, inner):
    owner = lax.rem(chunk, inner) * ch_count + chunk // inner
    return jnp.bitwise_xor(owner, member_index(ch_count, inner))


def conv_pack_kernel(inner, ch_count, cq_ref, ck_ref, cv_ref, cg_ref, *out_refs):
    rows = cq_ref.shape[0]
    piece = chunk_piece(pl.program_id(0), ch_count, inner)
    mixed = (ck_ref[...].astype(F32) * cv_ref[...].astype(F32)).astype(BF16)
    grad = (cg_ref[...].astype(F32) * cq_ref[...].astype(F32)).astype(BF16)
    for k, out_ref in enumerate(out_refs):

        @pl.when(piece == k)
        def _():
            out_ref[0:rows, :] = mixed
            out_ref[rows:, :] = grad


def conv_pack(cq, ck, cv, cg, inner, ch_count):
    rows, channels = cq.shape
    members = inner * ch_count
    width = channels // members
    spec = pl.BlockSpec((rows, width), lambda k: (0, k))
    return pl.pallas_call(
        functools.partial(conv_pack_kernel, inner, ch_count),
        grid=(members,),
        in_specs=[spec] * 4,
        out_specs=[pl.BlockSpec((2 * rows, width), lambda k: (0, 0))] * members,
        out_shape=[jax.ShapeDtypeStruct((2 * rows, width), BF16)] * members,
        cost_estimate=cost(4 * rows * channels, 12 * rows * channels),
        compiler_params=params(),
        name="conv_pack",
    )(cq, ck, cv, cg)


def conv_join_kernel(rows, inner, ch_count, *refs):
    members = inner * ch_count
    pieces, outs = refs[:members], refs[members:]
    half = members // 2
    me = member_index(ch_count, inner)
    for k, x_ref in enumerate(pieces):
        source = jnp.bitwise_xor(me, k)
        for part in range(2):

            @pl.when(source // half == part)
            def _():
                at = pl.multiple_of((source - part * half) * rows, rows)
                outs[part][pl.ds(at, rows), :] = x_ref[0:rows, :]
                outs[2 + part][pl.ds(at, rows), :] = x_ref[rows : 2 * rows, :]


def conv_join(pieces, rows, inner, ch_count):
    members, width = len(pieces), pieces[0].shape[1]
    step = min(width, 512)
    shape = jax.ShapeDtypeStruct((members * rows // 2, width), BF16)
    return pl.pallas_call(
        functools.partial(conv_join_kernel, rows, inner, ch_count),
        grid=(width // step,),
        in_specs=[pl.BlockSpec((2 * rows, step), lambda j: (0, j))] * members,
        out_specs=[pl.BlockSpec((members * rows // 2, step), lambda j: (0, j))] * 4,
        out_shape=[shape] * 4,
        cost_estimate=cost(0, 8 * members * rows * width),
        name="conv_join",
    )(*pieces)


def attn_pack_kernel(rows, q_ref, k_ref, v_ref, o_ref, g_ref, out_ref):
    heads = q_ref.shape[1] // HEAD_DIM
    span = LANES // rows
    offset = lax.rem(lax.axis_index("ch"), span) * rows
    product = g_ref[...].astype(F32) * o_ref[...].astype(F32)
    shape = (max(heads, 8), heads * HEAD_DIM)
    owner = lax.broadcasted_iota(jnp.int32, shape, 1) // HEAD_DIM
    chosen = (owner == lax.broadcasted_iota(jnp.int32, shape, 0)).astype(F32).astype(BF16)
    high, low = split_terms(product)
    delta = dot(chosen, high, NT) + dot(chosen, low, NT)
    delta = jnp.concatenate([delta, jnp.zeros((delta.shape[0], LANES - rows), F32)], axis=1)
    delta = pltpu.roll(delta, offset, 1)
    high = delta.astype(BF16).astype(F32)
    low = delta - high
    row = lax.broadcasted_iota(jnp.int32, (16, LANES), 0)
    for h in range(heads):
        cols = slice(h * HEAD_DIM, (h + 1) * HEAD_DIM)
        out_ref[h, 0:rows, :] = q_ref[:, cols]
        out_ref[h, rows : 2 * rows, :] = k_ref[:, cols]
        out_ref[h, 2 * rows : 3 * rows, :] = v_ref[:, cols]
        out_ref[h, 3 * rows : 4 * rows, :] = g_ref[:, cols]
        tile = jnp.where(row == 0, high[h : h + 1], jnp.where(row == 1, low[h : h + 1], 0.0))
        out_ref[h, 4 * rows : 4 * rows + 16, :] = tile.astype(BF16)


def attn_pack(q, k, v, o, g):
    rows, features = q.shape
    heads = features // HEAD_DIM
    step = math.gcd(heads, 16)
    spec = pl.BlockSpec((rows, step * HEAD_DIM), lambda j: (0, j))
    height = 4 * rows + 16
    return pl.pallas_call(
        functools.partial(attn_pack_kernel, rows),
        grid=(heads // step,),
        in_specs=[spec] * 5,
        out_specs=pl.BlockSpec((step, height, HEAD_DIM), lambda j: (j, 0, 0)),
        out_shape=jax.ShapeDtypeStruct((heads, height, HEAD_DIM), BF16),
        cost_estimate=cost(4 * rows * features, 20 * rows * features),
        name="attn_pack",
    )(q, k, v, o, g)


def attn_kernel(rows, reach, lens_ref, x_ref, out_ref, dk_ref, dv_ref):
    sources = x_ref.shape[0]
    per = LANES // rows
    blocks = sources // per
    scale = 1.0 / math.sqrt(HEAD_DIM)

    def part(first, count, which):
        return x_ref[first * per : (first + count) * per, which * rows : (which + 1) * rows, :].reshape(
            count * LANES, HEAD_DIM
        )

    dk_ref[...] = jnp.zeros_like(dk_ref)
    dv_ref[...] = jnp.zeros_like(dv_ref)
    for i in range(blocks):
        low = max(0, (i * LANES - (reach - 1)) // LANES)
        count = i + 1 - low
        query, grad = part(i, 1, 0), part(i, 1, 3)
        keys, values = part(low, count, 1), part(low, count, 2)
        delta = x_ref[i * per : (i + 1) * per, 4 * rows : 4 * rows + 16, :].astype(F32)
        delta = jnp.sum(jnp.sum(delta, axis=0), axis=0, keepdims=True)
        q_pos = i * LANES + lax.broadcasted_iota(jnp.int32, (8, LANES), 1)
        start = doc_start(lens_ref, q_pos)[0:1]
        k_pos = low * LANES + lax.broadcasted_iota(jnp.int32, (count * LANES, LANES), 0)
        visible = (k_pos >= start) & (k_pos <= q_pos[0:1])
        scores = jnp.where(visible, dot(keys, query, NT) * scale, NEG_FILL)
        top = jnp.max(scores, axis=0, keepdims=True)
        weights = jnp.where(visible, jnp.exp(scores - top), 0.0)
        probs = weights * (1.0 / jnp.sum(weights, axis=0, keepdims=True))
        grad_probs = dot(values, grad, NT)
        grad_scores = probs * (grad_probs - delta)
        span = slice(low * LANES, (i + 1) * LANES)
        p_terms = jnp.concatenate(split_terms(probs), axis=1)
        dv_ref[span, :] += dot(p_terms, jnp.concatenate([grad, grad], axis=0), NN)
        s_high, s_low = split_terms(grad_scores)
        s_terms = jnp.concatenate([s_high, s_low], axis=1)
        dk_ref[span, :] += dot(s_terms, jnp.concatenate([query, query], axis=0), NN)
        dq = dot(s_high, keys, TN) + dot(s_low, keys, TN)
        out_ref[i * per : (i + 1) * per, 0:rows, :] = (
            (dq * scale).astype(BF16).reshape(per, rows, HEAD_DIM)
        )
    for i in range(blocks):
        span = slice(i * LANES, (i + 1) * LANES)
        here = slice(i * per, (i + 1) * per)
        out_ref[here, rows : 2 * rows, :] = (
            (dk_ref[span, :] * scale).astype(BF16).reshape(per, rows, HEAD_DIM)
        )
        out_ref[here, 2 * rows : 3 * rows, :] = (
            dv_ref[span, :].astype(BF16).reshape(per, rows, HEAD_DIM)
        )


def attn_head(lens, x, rows, reach):
    sources = x.shape[0]
    tokens = sources * rows
    return pl.pallas_call(
        functools.partial(attn_kernel, rows, reach),
        in_specs=[
            pl.BlockSpec(memory_space=pltpu.SMEM),
            pl.BlockSpec(memory_space=pltpu.VMEM),
        ],
        out_specs=pl.BlockSpec(memory_space=pltpu.VMEM),
        out_shape=jax.ShapeDtypeStruct((sources, 3 * rows, HEAD_DIM), BF16),
        scratch_shapes=[
            pltpu.VMEM((tokens, HEAD_DIM), F32),
            pltpu.VMEM((tokens, HEAD_DIM), F32),
        ],
        cost_estimate=cost(tokens, x.size),
        name="attn_head",
    )(lens, x)


def attn_unpack_kernel(rows, x_ref, dq_ref, dk_ref, dv_ref):
    for h in range(x_ref.shape[0]):
        cols = slice(h * HEAD_DIM, (h + 1) * HEAD_DIM)
        dq_ref[:, cols] = x_ref[h, 0:rows, :]
        dk_ref[:, cols] = x_ref[h, rows : 2 * rows, :]
        dv_ref[:, cols] = x_ref[h, 2 * rows : 3 * rows, :]


def attn_unpack(x, rows):
    heads = x.shape[0]
    step = math.gcd(heads, 16)
    spec = pl.BlockSpec((rows, step * HEAD_DIM), lambda j: (0, j))
    shape = jax.ShapeDtypeStruct((rows, heads * HEAD_DIM), BF16)
    return pl.pallas_call(
        functools.partial(attn_unpack_kernel, rows),
        grid=(heads // step,),
        in_specs=[pl.BlockSpec((step, 3 * rows, HEAD_DIM), lambda j: (j, 0, 0))],
        out_specs=[spec] * 3,
        out_shape=[shape] * 3,
        cost_estimate=cost(0, 4 * x.size),
        compiler_params=params(),
        name="attn_unpack",
    )(x)


def circulant(row):
    rolled = pltpu.roll(jnp.broadcast_to(row, (8, LANES)), 0, 1, stride=1, stride_axis=0)
    pieces = [rolled if a == 0 else pltpu.roll(rolled, 8 * a, 1) for a in range(LANES // 8)]
    full = jnp.concatenate(pieces, axis=0).astype(BF16)
    return jnp.concatenate([full, full], axis=1)


def unskewed(outer):
    sub = lax.broadcasted_iota(jnp.int32, (8, LANES), 0)
    folded = outer[0:8]
    for a in range(1, LANES // 8):
        folded = folded + pltpu.roll(outer[8 * a : 8 * a + 8], LANES - 8 * a, 1)
    for bit in (1, 2, 4):
        folded = jnp.where((sub & bit) != 0, pltpu.roll(folded, LANES - bit, 1), folded)
    return jnp.sum(folded, axis=0, keepdims=True)


def reached(lens_ref, out_pos, in_pos):
    gap = out_pos - in_pos
    near = (gap >= 0) & (gap < FILTER_LEN) & (in_pos >= doc_start(lens_ref, out_pos))
    return near.astype(F32).astype(BF16)


def window_positions(inner, span):
    base = (lax.axis_index("seq") // inner) * span
    shape = (LANES, 2 * LANES)
    return (
        base + lax.broadcasted_iota(jnp.int32, shape, 0),
        base + lax.broadcasted_iota(jnp.int32, shape, 1),
    )


def conv_core_kernel(
    rows, inner, ch_count, lens_ref, tap_ref, rev_ref, prior_ref, m0_ref, m1_ref, g0_ref, g1_ref,
    later_ref, *refs,
):
    members = inner * ch_count
    outs = refs[:members]
    conv_ref, down_ref = refs[members:]
    me = member_index(ch_count, inner)
    groups = LANES // GROUP
    blocks = 2
    down, across = window_positions(inner, members * rows)
    back = [reached(lens_ref, down + b * LANES, across + (b - 1) * LANES) for b in range(blocks)]
    front = [reached(lens_ref, across + b * LANES, down + b * LANES) for b in range(blocks)]

    for tile in range(m0_ref.shape[1] // LANES):
        cols = slice(tile * LANES, (tile + 1) * LANES)
        mixed = [r[:, cols] for r in (prior_ref, m0_ref, m1_ref)]
        grad = [r[:, cols] for r in (g0_ref, g1_ref, later_ref)]
        lane_group = lax.broadcasted_iota(jnp.int32, (LANES, LANES), 1) // GROUP
        tap_rows = slice(tile * groups, (tile + 1) * groups)
        taps, rev_taps = tap_ref[tap_rows, :], rev_ref[tap_rows, :]
        back_taps = [circulant(rev_taps[g : g + 1]) for g in range(groups)]
        front_taps = [circulant(taps[g : g + 1]) for g in range(groups)]
        for b in range(blocks):
            window = jnp.concatenate(mixed[b : b + 2], axis=0)
            ahead = jnp.concatenate(grad[b : b + 2], axis=0)
            conv_all = dot(jnp.concatenate([t * back[b] for t in back_taps], axis=0), window, NN)
            down_all = dot(jnp.concatenate([t * front[b] for t in front_taps], axis=0), ahead, NN)
            conv_out = jnp.zeros((LANES, LANES), F32)
            mixed_grad = jnp.zeros((LANES, LANES), F32)
            for g in range(groups):
                mine = lane_group == g
                span = slice(g * LANES, (g + 1) * LANES)
                conv_out = jnp.where(mine, conv_all[span], conv_out)
                mixed_grad = jnp.where(mine, down_all[span], mixed_grad)
            here = slice(b * LANES, (b + 1) * LANES)
            conv_ref[here, cols] = conv_out.astype(BF16)
            down_ref[here, cols] = mixed_grad.astype(BF16)
    for k, out_ref in enumerate(outs):
        at = pl.multiple_of(jnp.bitwise_xor(me, k) * rows, rows)
        out_ref[0:rows, :] = conv_ref[pl.ds(at, rows), :]
        out_ref[rows : 2 * rows, :] = down_ref[pl.ds(at, rows), :]


def conv_core(lens, taps, rev_taps, arrays, rows, inner, ch_count):
    members = inner * ch_count
    width = arrays[0].shape[1]
    vmem = pl.BlockSpec(memory_space=pltpu.VMEM)
    return pl.pallas_call(
        functools.partial(conv_core_kernel, rows, inner, ch_count),
        in_specs=[pl.BlockSpec(memory_space=pltpu.SMEM)] + [vmem] * 8,
        out_specs=[vmem] * members,
        out_shape=[jax.ShapeDtypeStruct((2 * rows, width), BF16)] * members,
        scratch_shapes=[pltpu.VMEM((2 * LANES, width), BF16)] * 2,
        cost_estimate=cost(2000 * LANES * LANES * width, 24 * LANES * width),
        name="conv_core",
    )(lens, taps, rev_taps, *arrays)


def conv_filter_kernel(
    rows, inner, ch_count, lens_ref, prior_ref, m0_ref, m1_ref, g0_ref, g1_ref, filt_ref
):
    groups = LANES // GROUP
    blocks = 2
    down, across = window_positions(inner, inner * ch_count * rows)
    back = [
        reached(lens_ref, down + b * LANES, across + (b - 1) * LANES).astype(F32)
        for b in range(blocks)
    ]
    for tile in range(m0_ref.shape[1] // LANES):
        cols = slice(tile * LANES, (tile + 1) * LANES)
        mixed = [r[:, cols] for r in (prior_ref, m0_ref, m1_ref)]
        grad = [r[:, cols] for r in (g0_ref, g1_ref)]
        lane_group = lax.broadcasted_iota(jnp.int32, (LANES, LANES), 1) // GROUP
        sums = []
        for g in range(groups):
            mine = (lane_group == g).astype(F32).astype(BF16)
            outer = jnp.zeros((LANES, LANES), F32)
            for b in range(blocks):
                window = jnp.concatenate(mixed[b : b + 2], axis=0)
                full = dot(grad[b] * mine, window, NT) * back[b]
                outer = outer + full[:, 0:LANES] + full[:, LANES:]
            sums.append(unskewed(outer))
        filt_ref[tile * groups : (tile + 1) * groups, :] = jnp.concatenate(sums, axis=0)


def conv_filter_grad(lens, arrays, rows, inner, ch_count):
    width = arrays[0].shape[1]
    vmem = pl.BlockSpec(memory_space=pltpu.VMEM)
    return pl.pallas_call(
        functools.partial(conv_filter_kernel, rows, inner, ch_count),
        in_specs=[pl.BlockSpec(memory_space=pltpu.SMEM)] + [vmem] * 5,
        out_specs=vmem,
        out_shape=jax.ShapeDtypeStruct((width // GROUP, FILTER_LEN), F32),
        cost_estimate=cost(32 * LANES * LANES * width, 10 * LANES * width),
        name="conv_filter_grad",
    )(lens, *arrays)


def conv_unpack_kernel(inner, ch_count, each, ck_ref, cv_ref, cg_ref, *refs):
    members = inner * ch_count
    pieces, (gq_ref, gk_ref, gv_ref) = refs[:members], refs[members:]
    rows, width = pieces[0].shape[0] // 2, pieces[0].shape[1]
    for part in range(each):
        piece = chunk_piece(pl.program_id(0) * each + part, ch_count, inner)
        cols = slice(part * width, (part + 1) * width)
        for k, x_ref in enumerate(pieces):

            @pl.when(piece == k)
            def _():
                conv_out = x_ref[0:rows, :].astype(F32)
                mixed_grad = x_ref[rows : 2 * rows, :].astype(F32)
                gq_ref[:, cols] = (cg_ref[:, cols].astype(F32) * conv_out).astype(BF16)
                gk_ref[:, cols] = (mixed_grad * cv_ref[:, cols].astype(F32)).astype(BF16)
                gv_ref[:, cols] = (mixed_grad * ck_ref[:, cols].astype(F32)).astype(BF16)


def conv_unpack(pieces, ck, cv, cg, inner, ch_count):
    rows, channels = ck.shape
    members = inner * ch_count
    each = EACH
    width = each * channels // members
    spec = pl.BlockSpec((rows, width), lambda k: (0, k))
    shape = jax.ShapeDtypeStruct((rows, channels), BF16)
    return pl.pallas_call(
        functools.partial(conv_unpack_kernel, inner, ch_count, each),
        grid=(members // each,),
        in_specs=[spec] * 3 + [pl.BlockSpec(pieces[0].shape, lambda k: (0, 0))] * members,
        out_specs=[spec] * 3,
        out_shape=[shape] * 3,
        compiler_params=params(),
        cost_estimate=cost(6 * rows * channels, 16 * rows * channels),
        name="conv_unpack",
    )(ck, cv, cg, *pieces)


def doc_index(doc_lengths, positions):
    doc_ends = jnp.cumsum(doc_lengths)
    return jnp.sum((doc_ends[None, :] <= positions[:, None]).astype(jnp.int32), axis=1)


def split_rows(advance, carried, pieces):
    def one_block(block_index, current):
        sub_parts = tuple(
            lax.dynamic_slice_in_dim(part, block_index * 512, 512, 0) for part in pieces
        )
        return advance(current, sub_parts, block_index * 512)

    return lax.fori_loop(0, pieces[0].shape[0] // 512, one_block, carried)


def attn_gathered(attn_query, attn_key, attn_value, attn_output, attn_grad_out, doc_lengths):
    query_rows, key_rows, value_rows, output_rows, grad_rows = (
        lax.all_to_all(a, "ch", split_axis=1, concat_axis=0, tiled=True)
        for a in (attn_query, attn_key, attn_value, attn_output, attn_grad_out)
    )
    tok_rows = query_rows.shape[0]
    head_count = query_rows.shape[1] // HEAD_DIM
    scale_factor = 1.0 / math.sqrt(HEAD_DIM)
    local_pos = lax.axis_index("seq") * tok_rows + jnp.arange(tok_rows, dtype=jnp.int32)
    local_doc = doc_index(doc_lengths, local_pos)
    query_heads, key_heads, value_heads, output_heads, grad_heads = (
        a.reshape(tok_rows, head_count, HEAD_DIM)
        for a in (query_rows, key_rows, value_rows, output_rows, grad_rows)
    )
    delta_rows = jnp.sum(grad_heads.astype(F32) * output_heads.astype(F32), axis=2)
    delta_heads = delta_rows.T

    def key_step(carried, pieces, key_start):
        key_part, value_part = pieces
        key_pos = key_start + jnp.arange(key_part.shape[0], dtype=jnp.int32)
        key_doc = doc_index(doc_lengths, key_pos)
        visible = (key_doc[None, :] == local_doc[:, None]) & (key_pos[None, :] <= local_pos[:, None])
        running_max, running_sum, running_grad = carried
        scores = (
            jnp.einsum("thd,rhd->htr", query_heads, key_part, preferred_element_type=F32)
            * scale_factor
        )
        new_max = jnp.maximum(
            running_max, jnp.max(jnp.where(visible[None], scores, NEG_FILL), axis=2)
        )
        weights = jnp.where(visible[None], jnp.exp(scores - new_max[:, :, None]), 0.0)
        rescale = jnp.exp(running_max - new_max)
        grad_probs = jnp.einsum(
            "thd,rhd->htr", grad_heads, value_part, preferred_element_type=F32
        )
        weighted = weights * (grad_probs - delta_heads[:, :, None])
        update = jnp.einsum(
            "htr,rhd->htd", weighted, key_part.astype(F32), precision=lax.Precision.HIGHEST
        )
        return (
            new_max,
            running_sum * rescale + jnp.sum(weights, axis=2),
            running_grad * rescale[:, :, None] + update,
        )

    start_state = (
        jnp.full((head_count, tok_rows), NEG_FILL, F32),
        jnp.zeros((head_count, tok_rows), F32),
        jnp.zeros((head_count, tok_rows, HEAD_DIM), F32),
    )
    final_max, final_sum, final_grad = split_rows(
        key_step,
        start_state,
        (
            lax.all_gather(key_heads, "seq", axis=0, tiled=True),
            lax.all_gather(value_heads, "seq", axis=0, tiled=True),
        ),
    )
    lse_rows = (final_max + jnp.log(final_sum)).T
    grad_query = (final_grad * (scale_factor / final_sum)[:, :, None]).transpose(1, 0, 2)
    lse_whole = lax.all_gather(lse_rows, "seq", axis=0, tiled=True)
    delta_whole = lax.all_gather(delta_rows, "seq", axis=0, tiled=True)

    def query_step(carried, pieces, query_start):
        query_part, grad_part = pieces
        part_rows = query_part.shape[0]
        lse_part = lax.dynamic_slice_in_dim(lse_whole, query_start, part_rows, 0)
        delta_part = lax.dynamic_slice_in_dim(delta_whole, query_start, part_rows, 0)
        query_pos = query_start + jnp.arange(part_rows, dtype=jnp.int32)
        query_doc = doc_index(doc_lengths, query_pos)
        visible = (query_doc[:, None] == local_doc[None, :]) & (
            local_pos[None, :] <= query_pos[:, None]
        )
        key_grad, value_grad = carried
        scores = (
            jnp.einsum("rhd,thd->hrt", query_part, key_heads, preferred_element_type=F32)
            * scale_factor
        )
        probs = jnp.where(visible[None], jnp.exp(scores - lse_part.T[:, :, None]), 0.0)
        value_grad = value_grad + jnp.einsum(
            "hrt,rhd->thd", probs, grad_part.astype(F32), precision=lax.Precision.HIGHEST
        )
        grad_probs = jnp.einsum(
            "rhd,thd->hrt", grad_part, value_heads, preferred_element_type=F32
        )
        grad_scores = probs * (grad_probs - delta_part.T[:, :, None])
        key_grad = key_grad + scale_factor * jnp.einsum(
            "hrt,rhd->thd", grad_scores, query_part.astype(F32), precision=lax.Precision.HIGHEST
        )
        return (key_grad, value_grad)

    zero = jnp.zeros((tok_rows, head_count, HEAD_DIM), F32)
    key_grad, value_grad = split_rows(
        query_step,
        (zero, zero),
        (
            lax.all_gather(query_heads, "seq", axis=0, tiled=True),
            lax.all_gather(grad_heads, "seq", axis=0, tiled=True),
        ),
    )
    return tuple(
        lax.all_to_all(
            a.reshape(tok_rows, head_count * HEAD_DIM).astype(BF16),
            "ch",
            split_axis=0,
            concat_axis=1,
            tiled=True,
        )
        for a in (grad_query, key_grad, value_grad)
    )


def shifted(block, distance, count):
    route = [(i, i + distance) for i in range(count) if 0 <= i + distance < count]
    return lax.ppermute(block, DEVICES, route)


def exchanged(block, distance, count):
    return lax.ppermute(block, DEVICES, [(i, i ^ distance) for i in range(count)])


def body(
    attn_query, attn_key, attn_value, attn_output, attn_grad_out,
    conv_query, conv_key, conv_value, conv_grad_out, conv_filter, doc_lengths,
):
    seq_count, ch_count = lax.axis_size("seq"), lax.axis_size("ch")
    count = seq_count * ch_count
    rows, channels = conv_query.shape
    inner = 2
    members = inner * ch_count
    outer = seq_count // inner
    heads = attn_query.shape[1] // HEAD_DIM
    head_each = heads == count

    reach = BAND_REACH if rows * count == 1024 else rows * count

    if head_each:
        attn_packed = attn_pack(attn_query, attn_key, attn_value, attn_output, attn_grad_out)
        attn_in = lax.all_to_all(attn_packed, DEVICES, split_axis=0, concat_axis=0, tiled=True)

    packed = conv_pack(conv_query, conv_key, conv_value, conv_grad_out, inner, ch_count)
    pieces = [packed[0]] + [exchanged(packed[k], k, count) for k in range(1, members)]
    group_count = channels // members // GROUP
    y = lax.rem(lax.axis_index("seq"), inner)
    taps = lax.dynamic_slice_in_dim(conv_filter, y * group_count, group_count, 0).astype(F32)
    rev_taps = jnp.roll(taps[:, ::-1], 1, axis=1)
    taps, rev_taps, *pieces = lax.optimization_barrier((taps, rev_taps, *pieces))
    mixed_lo, mixed_hi, grad_lo, grad_hi = conv_join(pieces, rows, inner, ch_count)
    if head_each:
        attn_in, mixed_hi, grad_lo = lax.optimization_barrier((attn_in, mixed_hi, grad_lo))
    prior, later = shifted(mixed_hi, members, count), shifted(grad_lo, -members, count)
    if head_each:
        attn_back = attn_head(doc_lengths, attn_in, rows, reach)
        attn_back, taps, rev_taps = lax.optimization_barrier((attn_back, taps, rev_taps))
        attn_res = lax.all_to_all(attn_back, DEVICES, split_axis=0, concat_axis=0, tiled=True)
    own = (prior, mixed_lo, mixed_hi, grad_lo, grad_hi, later)
    filter_part = conv_filter_grad(doc_lengths, own[:5], rows, inner, ch_count)
    other = exchanged(filter_part, members, count)
    taps, filter_part = lax.optimization_barrier((taps, filter_part))
    conv_back = conv_core(doc_lengths, taps, rev_taps, own, rows, inner, ch_count)
    other, *conv_back = lax.optimization_barrier((other, *conv_back))
    conv_res = [conv_back[0]] + [exchanged(conv_back[k], k, count) for k in range(1, members)]
    filter_part = filter_part + other
    filter_part, conv_res[1:4] = lax.optimization_barrier((filter_part, conv_res[1:4]))
    distance = 2 * members
    while distance < count:
        other = exchanged(filter_part, distance, count)
        conv_res, other = lax.optimization_barrier((conv_res, other))
        filter_part = filter_part + other
        distance *= 2
    filter_part = jnp.roll(filter_part[:, ::-1], 1, axis=1)
    other = exchanged(filter_part, ch_count, count)
    grad_conv = conv_unpack(conv_res, conv_key, conv_value, conv_grad_out, inner, ch_count)
    if head_each:
        grad_attn = attn_unpack(attn_res, rows)
        other, *grad_attn = lax.optimization_barrier((other, *grad_attn))
    else:
        grad_attn = attn_gathered(
            attn_query, attn_key, attn_value, attn_output, attn_grad_out, doc_lengths
        )
    other, *grad_conv = lax.optimization_barrier((other, *grad_conv))
    grad_filter = jnp.where(
        y == 0,
        jnp.concatenate([filter_part, other], axis=0),
        jnp.concatenate([other, filter_part], axis=0),
    )
    return (*grad_attn, *grad_conv, grad_filter)


def solution(mesh):
    rows = P(("seq", "ch"), None)
    return jax.shard_map(
        body,
        mesh=mesh,
        in_specs=(rows,) * 9 + (P("ch", None), P()),
        out_specs=(rows,) * 6 + (P("ch", None),),
        check_vma=False,
    )
```

```python
import functools
import math

import jax
import jax.numpy as jnp
from jax import lax
from jax.experimental import pallas as pl
from jax.experimental.pallas import tpu as pltpu
from jax.sharding import PartitionSpec as P

HEAD_DIM = 128
GROUP = 16
FILTER_LEN = 128
LANES = 128
EACH = 2
BAND_REACH = 320
DEVICES = ("seq", "ch")
NEG_FILL = -1e30
BF16 = jnp.bfloat16
F32 = jnp.float32

NT = (((1,), (1,)), ((), ()))
NN = (((1,), (0,)), ((), ()))
TN = (((0,), (0,)), ((), ()))


def dot(a, b, dims):
    return lax.dot_general(a, b, dims, preferred_element_type=F32)


def params():
    return pltpu.CompilerParams(vmem_limit_bytes=40 * 1024 * 1024)


def cost(flops, bytes_accessed):
    return pl.CostEstimate(flops=flops, bytes_accessed=bytes_accessed, transcendentals=0)


def split_terms(x):
    high = x.astype(BF16)
    low = (x - high.astype(F32)).astype(BF16)
    return high, low


def doc_start(lens_ref, positions):
    start = jnp.zeros_like(positions)
    end = jnp.int32(0)
    for d in range(lens_ref.shape[0]):
        end = end + lens_ref[d]
        start = jnp.where(positions >= end, end, start)
    return start


def member_index(ch_count, inner):
    return lax.rem(lax.axis_index("seq"), inner) * ch_count + lax.axis_index("ch")


def chunk_piece(chunk, ch_count, inner):
    owner = lax.rem(chunk, inner) * ch_count + chunk // inner
    return jnp.bitwise_xor(owner, member_index(ch_count, inner))


def conv_pack_kernel(inner, ch_count, cq_ref, ck_ref, cv_ref, cg_ref, *out_refs):
    rows = cq_ref.shape[0]
    piece = chunk_piece(pl.program_id(0), ch_count, inner)
    mixed = (ck_ref[...].astype(F32) * cv_ref[...].astype(F32)).astype(BF16)
    grad = (cg_ref[...].astype(F32) * cq_ref[...].astype(F32)).astype(BF16)
    for k, out_ref in enumerate(out_refs):

        @pl.when(piece == k)
        def _():
            out_ref[0:rows, :] = mixed
            out_ref[rows:, :] = grad


def conv_pack(cq, ck, cv, cg, inner, ch_count):
    rows, channels = cq.shape
    members = inner * ch_count
    width = channels // members
    spec = pl.BlockSpec((rows, width), lambda k: (0, k))
    return pl.pallas_call(
        functools.partial(conv_pack_kernel, inner, ch_count),
        grid=(members,),
        in_specs=[spec] * 4,
        out_specs=[pl.BlockSpec((2 * rows, width), lambda k: (0, 0))] * members,
        out_shape=[jax.ShapeDtypeStruct((2 * rows, width), BF16)] * members,
        cost_estimate=cost(4 * rows * channels, 12 * rows * channels),
        compiler_params=params(),
        name="conv_pack",
    )(cq, ck, cv, cg)


def conv_join_kernel(rows, inner, ch_count, *refs):
    members = inner * ch_count
    pieces, outs = refs[:members], refs[members:]
    half = members // 2
    me = member_index(ch_count, inner)
    for k, x_ref in enumerate(pieces):
        source = jnp.bitwise_xor(me, k)
        for part in range(2):

            @pl.when(source // half == part)
            def _():
                at = pl.multiple_of((source - part * half) * rows, rows)
                outs[part][pl.ds(at, rows), :] = x_ref[0:rows, :]
                outs[2 + part][pl.ds(at, rows), :] = x_ref[rows : 2 * rows, :]


def conv_join(pieces, rows, inner, ch_count):
    members, width = len(pieces), pieces[0].shape[1]
    step = min(width, 512)
    shape = jax.ShapeDtypeStruct((members * rows // 2, width), BF16)
    return pl.pallas_call(
        functools.partial(conv_join_kernel, rows, inner, ch_count),
        grid=(width // step,),
        in_specs=[pl.BlockSpec((2 * rows, step), lambda j: (0, j))] * members,
        out_specs=[pl.BlockSpec((members * rows // 2, step), lambda j: (0, j))] * 4,
        out_shape=[shape] * 4,
        cost_estimate=cost(0, 8 * members * rows * width),
        name="conv_join",
    )(*pieces)


def attn_pack_kernel(rows, q_ref, k_ref, v_ref, o_ref, g_ref, out_ref):
    heads = q_ref.shape[1] // HEAD_DIM
    span = LANES // rows
    offset = lax.rem(lax.axis_index("ch"), span) * rows
    product = g_ref[...].astype(F32) * o_ref[...].astype(F32)
    shape = (max(heads, 8), heads * HEAD_DIM)
    owner = lax.broadcasted_iota(jnp.int32, shape, 1) // HEAD_DIM
    chosen = (owner == lax.broadcasted_iota(jnp.int32, shape, 0)).astype(F32).astype(BF16)
    high, low = split_terms(product)
    delta = dot(chosen, high, NT) + dot(chosen, low, NT)
    delta = jnp.concatenate([delta, jnp.zeros((delta.shape[0], LANES - rows), F32)], axis=1)
    delta = pltpu.roll(delta, offset, 1)
    high = delta.astype(BF16).astype(F32)
    low = delta - high
    row = lax.broadcasted_iota(jnp.int32, (16, LANES), 0)
    for h in range(heads):
        cols = slice(h * HEAD_DIM, (h + 1) * HEAD_DIM)
        out_ref[h, 0:rows, :] = q_ref[:, cols]
        out_ref[h, rows : 2 * rows, :] = k_ref[:, cols]
        out_ref[h, 2 * rows : 3 * rows, :] = v_ref[:, cols]
        out_ref[h, 3 * rows : 4 * rows, :] = g_ref[:, cols]
        tile = jnp.where(row == 0, high[h : h + 1], jnp.where(row == 1, low[h : h + 1], 0.0))
        out_ref[h, 4 * rows : 4 * rows + 16, :] = tile.astype(BF16)


def attn_pack(q, k, v, o, g):
    rows, features = q.shape
    heads = features // HEAD_DIM
    step = math.gcd(heads, 16)
    spec = pl.BlockSpec((rows, step * HEAD_DIM), lambda j: (0, j))
    height = 4 * rows + 16
    return pl.pallas_call(
        functools.partial(attn_pack_kernel, rows),
        grid=(heads // step,),
        in_specs=[spec] * 5,
        out_specs=pl.BlockSpec((step, height, HEAD_DIM), lambda j: (j, 0, 0)),
        out_shape=jax.ShapeDtypeStruct((heads, height, HEAD_DIM), BF16),
        cost_estimate=cost(4 * rows * features, 20 * rows * features),
        name="attn_pack",
    )(q, k, v, o, g)


def attn_kernel(rows, reach, lens_ref, x_ref, out_ref, dk_ref, dv_ref):
    sources = x_ref.shape[0]
    per = LANES // rows
    blocks = sources // per
    scale = 1.0 / math.sqrt(HEAD_DIM)

    def part(first, count, which):
        return x_ref[first * per : (first + count) * per, which * rows : (which + 1) * rows, :].reshape(
            count * LANES, HEAD_DIM
        )

    dk_ref[...] = jnp.zeros_like(dk_ref)
    dv_ref[...] = jnp.zeros_like(dv_ref)
    for i in range(blocks):
        low = max(0, (i * LANES - (reach - 1)) // LANES)
        count = i + 1 - low
        query, grad = part(i, 1, 0), part(i, 1, 3)
        keys, values = part(low, count, 1), part(low, count, 2)
        delta = x_ref[i * per : (i + 1) * per, 4 * rows : 4 * rows + 16, :].astype(F32)
        delta = jnp.sum(jnp.sum(delta, axis=0), axis=0, keepdims=True)
        q_pos = i * LANES + lax.broadcasted_iota(jnp.int32, (8, LANES), 1)
        start = doc_start(lens_ref, q_pos)[0:1]
        k_pos = low * LANES + lax.broadcasted_iota(jnp.int32, (count * LANES, LANES), 0)
        visible = (k_pos >= start) & (k_pos <= q_pos[0:1])
        scores = jnp.where(visible, dot(keys, query, NT) * scale, NEG_FILL)
        top = jnp.max(scores, axis=0, keepdims=True)
        weights = jnp.where(visible, jnp.exp(scores - top), 0.0)
        probs = weights * (1.0 / jnp.sum(weights, axis=0, keepdims=True))
        grad_probs = dot(values, grad, NT)
        grad_scores = probs * (grad_probs - delta)
        span = slice(low * LANES, (i + 1) * LANES)
        p_terms = jnp.concatenate(split_terms(probs), axis=1)
        dv_ref[span, :] += dot(p_terms, jnp.concatenate([grad, grad], axis=0), NN)
        s_high, s_low = split_terms(grad_scores)
        s_terms = jnp.concatenate([s_high, s_low], axis=1)
        dk_ref[span, :] += dot(s_terms, jnp.concatenate([query, query], axis=0), NN)
        dq = dot(s_high, keys, TN) + dot(s_low, keys, TN)
        out_ref[i * per : (i + 1) * per, 0:rows, :] = (
            (dq * scale).astype(BF16).reshape(per, rows, HEAD_DIM)
        )
    for i in range(blocks):
        span = slice(i * LANES, (i + 1) * LANES)
        here = slice(i * per, (i + 1) * per)
        out_ref[here, rows : 2 * rows, :] = (
            (dk_ref[span, :] * scale).astype(BF16).reshape(per, rows, HEAD_DIM)
        )
        out_ref[here, 2 * rows : 3 * rows, :] = (
            dv_ref[span, :].astype(BF16).reshape(per, rows, HEAD_DIM)
        )


def attn_head(lens, x, rows, reach):
    sources = x.shape[0]
    tokens = sources * rows
    return pl.pallas_call(
        functools.partial(attn_kernel, rows, reach),
        in_specs=[
            pl.BlockSpec(memory_space=pltpu.SMEM),
            pl.BlockSpec(memory_space=pltpu.VMEM),
        ],
        out_specs=pl.BlockSpec(memory_space=pltpu.VMEM),
        out_shape=jax.ShapeDtypeStruct((sources, 3 * rows, HEAD_DIM), BF16),
        scratch_shapes=[
            pltpu.VMEM((tokens, HEAD_DIM), F32),
            pltpu.VMEM((tokens, HEAD_DIM), F32),
        ],
        cost_estimate=cost(tokens, x.size),
        compiler_params=pltpu.CompilerParams(vmem_limit_bytes=40 * 1024 * 1024),
        name="attn_head",
    )(lens, x)


def attn_unpack_kernel(rows, inner, x_ref, mine_ref, other_ref, dq_ref, dk_ref, dv_ref, filt_ref):
    for h in range(x_ref.shape[0]):
        cols = slice(h * HEAD_DIM, (h + 1) * HEAD_DIM)
        dq_ref[:, cols] = x_ref[h, 0:rows, :]
        dk_ref[:, cols] = x_ref[h, rows : 2 * rows, :]
        dv_ref[:, cols] = x_ref[h, 2 * rows : 3 * rows, :]

    @pl.when(pl.program_id(0) == 0)
    def _():
        groups = mine_ref.shape[0]
        at = lax.rem(lax.axis_index("seq"), inner) * groups
        filt_ref[pl.ds(pl.multiple_of(at, groups), groups), :] = mine_ref[...]
        at = groups - at
        filt_ref[pl.ds(pl.multiple_of(at, groups), groups), :] = other_ref[...]


def attn_unpack(x, mine, other, rows, inner):
    heads = x.shape[0]
    step = math.gcd(heads, 16)
    spec = pl.BlockSpec((rows, step * HEAD_DIM), lambda j: (0, j))
    half = pl.BlockSpec(mine.shape, lambda j: (0, 0))
    whole = (2 * mine.shape[0], mine.shape[1])
    shape = jax.ShapeDtypeStruct((rows, heads * HEAD_DIM), BF16)
    return pl.pallas_call(
        functools.partial(attn_unpack_kernel, rows, inner),
        grid=(heads // step,),
        in_specs=[pl.BlockSpec((step, 3 * rows, HEAD_DIM), lambda j: (j, 0, 0)), half, half],
        out_specs=[spec] * 3 + [pl.BlockSpec(whole, lambda j: (0, 0))],
        out_shape=[shape] * 3 + [jax.ShapeDtypeStruct(whole, F32)],
        compiler_params=params(),
        cost_estimate=cost(0, 4 * x.size),
        name="attn_unpack",
    )(x, mine, other)


def circulant(row):
    rolled = pltpu.roll(jnp.broadcast_to(row, (8, LANES)), 0, 1, stride=1, stride_axis=0)
    pieces = [rolled if a == 0 else pltpu.roll(rolled, 8 * a, 1) for a in range(LANES // 8)]
    full = jnp.concatenate(pieces, axis=0).astype(BF16)
    return jnp.concatenate([full, full], axis=1)


def unskewed(outer):
    sub = lax.broadcasted_iota(jnp.int32, (8, LANES), 0)
    folded = outer[0:8]
    for a in range(1, LANES // 8):
        folded = folded + pltpu.roll(outer[8 * a : 8 * a + 8], LANES - 8 * a, 1)
    for bit in (1, 2, 4):
        folded = jnp.where((sub & bit) != 0, pltpu.roll(folded, LANES - bit, 1), folded)
    return jnp.sum(folded, axis=0, keepdims=True)


def reached(lens_ref, out_pos, in_pos):
    gap = out_pos - in_pos
    near = (gap >= 0) & (gap < FILTER_LEN) & (in_pos >= doc_start(lens_ref, out_pos))
    return near.astype(F32).astype(BF16)


def window_positions(inner, span):
    base = (lax.axis_index("seq") // inner) * span
    shape = (LANES, 2 * LANES)
    return (
        base + lax.broadcasted_iota(jnp.int32, shape, 0),
        base + lax.broadcasted_iota(jnp.int32, shape, 1),
    )


def conv_core_kernel(
    rows, inner, ch_count, lens_ref, tap_ref, rev_ref, prior_ref, m0_ref, m1_ref, g0_ref, g1_ref,
    later_ref, *refs,
):
    members = inner * ch_count
    outs = refs[:members]
    conv_ref, down_ref = refs[members:]
    me = member_index(ch_count, inner)
    groups = LANES // GROUP
    blocks = 2
    down, across = window_positions(inner, members * rows)
    back = [reached(lens_ref, down + b * LANES, across + (b - 1) * LANES) for b in range(blocks)]
    front = [reached(lens_ref, across + b * LANES, down + b * LANES) for b in range(blocks)]

    for tile in range(m0_ref.shape[1] // LANES):
        cols = slice(tile * LANES, (tile + 1) * LANES)
        mixed = [r[:, cols] for r in (prior_ref, m0_ref, m1_ref)]
        grad = [r[:, cols] for r in (g0_ref, g1_ref, later_ref)]
        lane_group = lax.broadcasted_iota(jnp.int32, (LANES, LANES), 1) // GROUP
        tap_rows = slice(tile * groups, (tile + 1) * groups)
        taps, rev_taps = tap_ref[tap_rows, :], rev_ref[tap_rows, :]
        back_taps = [circulant(rev_taps[g : g + 1]) for g in range(groups)]
        front_taps = [circulant(taps[g : g + 1]) for g in range(groups)]
        for b in range(blocks):
            window = jnp.concatenate(mixed[b : b + 2], axis=0)
            ahead = jnp.concatenate(grad[b : b + 2], axis=0)
            conv_all = dot(jnp.concatenate([t * back[b] for t in back_taps], axis=0), window, NN)
            down_all = dot(jnp.concatenate([t * front[b] for t in front_taps], axis=0), ahead, NN)
            conv_out = jnp.zeros((LANES, LANES), F32)
            mixed_grad = jnp.zeros((LANES, LANES), F32)
            for g in range(groups):
                mine = lane_group == g
                span = slice(g * LANES, (g + 1) * LANES)
                conv_out = jnp.where(mine, conv_all[span], conv_out)
                mixed_grad = jnp.where(mine, down_all[span], mixed_grad)
            here = slice(b * LANES, (b + 1) * LANES)
            conv_ref[here, cols] = conv_out.astype(BF16)
            down_ref[here, cols] = mixed_grad.astype(BF16)
    for k, out_ref in enumerate(outs):
        at = pl.multiple_of(jnp.bitwise_xor(me, k) * rows, rows)
        out_ref[0:rows, :] = conv_ref[pl.ds(at, rows), :]
        out_ref[rows : 2 * rows, :] = down_ref[pl.ds(at, rows), :]


def conv_core(lens, taps, rev_taps, arrays, rows, inner, ch_count):
    members = inner * ch_count
    width = arrays[0].shape[1]
    vmem = pl.BlockSpec(memory_space=pltpu.VMEM)
    return pl.pallas_call(
        functools.partial(conv_core_kernel, rows, inner, ch_count),
        in_specs=[pl.BlockSpec(memory_space=pltpu.SMEM)] + [vmem] * 8,
        out_specs=[vmem] * members,
        out_shape=[jax.ShapeDtypeStruct((2 * rows, width), BF16)] * members,
        scratch_shapes=[pltpu.VMEM((2 * LANES, width), BF16)] * 2,
        cost_estimate=cost(2000 * LANES * LANES * width, 24 * LANES * width),
        compiler_params=pltpu.CompilerParams(vmem_limit_bytes=40 * 1024 * 1024),
        name="conv_core",
    )(lens, taps, rev_taps, *arrays)


def conv_filter_kernel(
    rows, inner, ch_count, lens_ref, prior_ref, m0_ref, m1_ref, g0_ref, g1_ref, filt_ref
):
    groups = LANES // GROUP
    blocks = 2
    down, across = window_positions(inner, inner * ch_count * rows)
    back = [
        reached(lens_ref, down + b * LANES, across + (b - 1) * LANES).astype(F32)
        for b in range(blocks)
    ]
    for tile in range(m0_ref.shape[1] // LANES):
        cols = slice(tile * LANES, (tile + 1) * LANES)
        mixed = [r[:, cols] for r in (prior_ref, m0_ref, m1_ref)]
        grad = [r[:, cols] for r in (g0_ref, g1_ref)]
        lane_group = lax.broadcasted_iota(jnp.int32, (LANES, LANES), 1) // GROUP
        sums = []
        for g in range(groups):
            mine = (lane_group == g).astype(F32).astype(BF16)
            outer = jnp.zeros((LANES, LANES), F32)
            for b in range(blocks):
                window = jnp.concatenate(mixed[b : b + 2], axis=0)
                full = dot(grad[b] * mine, window, NT) * back[b]
                outer = outer + full[:, 0:LANES] + full[:, LANES:]
            sums.append(unskewed(outer))
        filt_ref[tile * groups : (tile + 1) * groups, :] = jnp.concatenate(sums, axis=0)


def conv_filter_grad(lens, arrays, rows, inner, ch_count):
    width = arrays[0].shape[1]
    vmem = pl.BlockSpec(memory_space=pltpu.VMEM)
    return pl.pallas_call(
        functools.partial(conv_filter_kernel, rows, inner, ch_count),
        in_specs=[pl.BlockSpec(memory_space=pltpu.SMEM)] + [vmem] * 5,
        out_specs=vmem,
        out_shape=jax.ShapeDtypeStruct((width // GROUP, FILTER_LEN), F32),
        cost_estimate=cost(32 * LANES * LANES * width, 10 * LANES * width),
        compiler_params=pltpu.CompilerParams(vmem_limit_bytes=40 * 1024 * 1024),
        name="conv_filter_grad",
    )(lens, *arrays)


def conv_unpack_kernel(inner, ch_count, each, ck_ref, cv_ref, cg_ref, *refs):
    members = inner * ch_count
    pieces, (gq_ref, gk_ref, gv_ref) = refs[:members], refs[members:]
    rows, width = pieces[0].shape[0] // 2, pieces[0].shape[1]
    for part in range(each):
        piece = chunk_piece(pl.program_id(0) * each + part, ch_count, inner)
        cols = slice(part * width, (part + 1) * width)
        for k, x_ref in enumerate(pieces):

            @pl.when(piece == k)
            def _():
                conv_out = x_ref[0:rows, :].astype(F32)
                mixed_grad = x_ref[rows : 2 * rows, :].astype(F32)
                gq_ref[:, cols] = (cg_ref[:, cols].astype(F32) * conv_out).astype(BF16)
                gk_ref[:, cols] = (mixed_grad * cv_ref[:, cols].astype(F32)).astype(BF16)
                gv_ref[:, cols] = (mixed_grad * ck_ref[:, cols].astype(F32)).astype(BF16)


def conv_unpack(pieces, ck, cv, cg, inner, ch_count):
    rows, channels = ck.shape
    members = inner * ch_count
    each = EACH
    width = each * channels // members
    spec = pl.BlockSpec((rows, width), lambda k: (0, k))
    shape = jax.ShapeDtypeStruct((rows, channels), BF16)
    return pl.pallas_call(
        functools.partial(conv_unpack_kernel, inner, ch_count, each),
        grid=(members // each,),
        in_specs=[spec] * 3 + [pl.BlockSpec(pieces[0].shape, lambda k: (0, 0))] * members,
        out_specs=[spec] * 3,
        out_shape=[shape] * 3,
        compiler_params=params(),
        cost_estimate=cost(6 * rows * channels, 16 * rows * channels),
        name="conv_unpack",
    )(ck, cv, cg, *pieces)


def doc_index(doc_lengths, positions):
    doc_ends = jnp.cumsum(doc_lengths)
    return jnp.sum((doc_ends[None, :] <= positions[:, None]).astype(jnp.int32), axis=1)


def split_rows(advance, carried, pieces):
    def one_block(block_index, current):
        sub_parts = tuple(
            lax.dynamic_slice_in_dim(part, block_index * 512, 512, 0) for part in pieces
        )
        return advance(current, sub_parts, block_index * 512)

    return lax.fori_loop(0, pieces[0].shape[0] // 512, one_block, carried)


def attn_gathered(attn_query, attn_key, attn_value, attn_output, attn_grad_out, doc_lengths):
    query_rows, key_rows, value_rows, output_rows, grad_rows = (
        lax.all_to_all(a, "ch", split_axis=1, concat_axis=0, tiled=True)
        for a in (attn_query, attn_key, attn_value, attn_output, attn_grad_out)
    )
    tok_rows = query_rows.shape[0]
    head_count = query_rows.shape[1] // HEAD_DIM
    scale_factor = 1.0 / math.sqrt(HEAD_DIM)
    local_pos = lax.axis_index("seq") * tok_rows + jnp.arange(tok_rows, dtype=jnp.int32)
    local_doc = doc_index(doc_lengths, local_pos)
    query_heads, key_heads, value_heads, output_heads, grad_heads = (
        a.reshape(tok_rows, head_count, HEAD_DIM)
        for a in (query_rows, key_rows, value_rows, output_rows, grad_rows)
    )
    delta_rows = jnp.sum(grad_heads.astype(F32) * output_heads.astype(F32), axis=2)
    delta_heads = delta_rows.T

    def key_step(carried, pieces, key_start):
        key_part, value_part = pieces
        key_pos = key_start + jnp.arange(key_part.shape[0], dtype=jnp.int32)
        key_doc = doc_index(doc_lengths, key_pos)
        visible = (key_doc[None, :] == local_doc[:, None]) & (key_pos[None, :] <= local_pos[:, None])
        running_max, running_sum, running_grad = carried
        scores = (
            jnp.einsum("thd,rhd->htr", query_heads, key_part, preferred_element_type=F32)
            * scale_factor
        )
        new_max = jnp.maximum(
            running_max, jnp.max(jnp.where(visible[None], scores, NEG_FILL), axis=2)
        )
        weights = jnp.where(visible[None], jnp.exp(scores - new_max[:, :, None]), 0.0)
        rescale = jnp.exp(running_max - new_max)
        grad_probs = jnp.einsum(
            "thd,rhd->htr", grad_heads, value_part, preferred_element_type=F32
        )
        weighted = weights * (grad_probs - delta_heads[:, :, None])
        update = jnp.einsum(
            "htr,rhd->htd", weighted, key_part.astype(F32), precision=lax.Precision.HIGHEST
        )
        return (
            new_max,
            running_sum * rescale + jnp.sum(weights, axis=2),
            running_grad * rescale[:, :, None] + update,
        )

    start_state = (
        jnp.full((head_count, tok_rows), NEG_FILL, F32),
        jnp.zeros((head_count, tok_rows), F32),
        jnp.zeros((head_count, tok_rows, HEAD_DIM), F32),
    )
    final_max, final_sum, final_grad = split_rows(
        key_step,
        start_state,
        (
            lax.all_gather(key_heads, "seq", axis=0, tiled=True),
            lax.all_gather(value_heads, "seq", axis=0, tiled=True),
        ),
    )
    lse_rows = (final_max + jnp.log(final_sum)).T
    grad_query = (final_grad * (scale_factor / final_sum)[:, :, None]).transpose(1, 0, 2)
    lse_whole = lax.all_gather(lse_rows, "seq", axis=0, tiled=True)
    delta_whole = lax.all_gather(delta_rows, "seq", axis=0, tiled=True)

    def query_step(carried, pieces, query_start):
        query_part, grad_part = pieces
        part_rows = query_part.shape[0]
        lse_part = lax.dynamic_slice_in_dim(lse_whole, query_start, part_rows, 0)
        delta_part = lax.dynamic_slice_in_dim(delta_whole, query_start, part_rows, 0)
        query_pos = query_start + jnp.arange(part_rows, dtype=jnp.int32)
        query_doc = doc_index(doc_lengths, query_pos)
        visible = (query_doc[:, None] == local_doc[None, :]) & (
            local_pos[None, :] <= query_pos[:, None]
        )
        key_grad, value_grad = carried
        scores = (
            jnp.einsum("rhd,thd->hrt", query_part, key_heads, preferred_element_type=F32)
            * scale_factor
        )
        probs = jnp.where(visible[None], jnp.exp(scores - lse_part.T[:, :, None]), 0.0)
        value_grad = value_grad + jnp.einsum(
            "hrt,rhd->thd", probs, grad_part.astype(F32), precision=lax.Precision.HIGHEST
        )
        grad_probs = jnp.einsum(
            "rhd,thd->hrt", grad_part, value_heads, preferred_element_type=F32
        )
        grad_scores = probs * (grad_probs - delta_part.T[:, :, None])
        key_grad = key_grad + scale_factor * jnp.einsum(
            "hrt,rhd->thd", grad_scores, query_part.astype(F32), precision=lax.Precision.HIGHEST
        )
        return (key_grad, value_grad)

    zero = jnp.zeros((tok_rows, head_count, HEAD_DIM), F32)
    key_grad, value_grad = split_rows(
        query_step,
        (zero, zero),
        (
            lax.all_gather(query_heads, "seq", axis=0, tiled=True),
            lax.all_gather(grad_heads, "seq", axis=0, tiled=True),
        ),
    )
    return tuple(
        lax.all_to_all(
            a.reshape(tok_rows, head_count * HEAD_DIM).astype(BF16),
            "ch",
            split_axis=0,
            concat_axis=1,
            tiled=True,
        )
        for a in (grad_query, key_grad, value_grad)
    )


def shifted(block, distance, count):
    route = [(i, i + distance) for i in range(count) if 0 <= i + distance < count]
    return lax.ppermute(block, DEVICES, route)


def exchanged(block, distance, count):
    return lax.ppermute(block, DEVICES, [(i, i ^ distance) for i in range(count)])


def body(
    attn_query, attn_key, attn_value, attn_output, attn_grad_out,
    conv_query, conv_key, conv_value, conv_grad_out, conv_filter, doc_lengths,
):
    seq_count, ch_count = lax.axis_size("seq"), lax.axis_size("ch")
    count = seq_count * ch_count
    rows, channels = conv_query.shape
    inner = 2
    members = inner * ch_count
    outer = seq_count // inner
    heads = attn_query.shape[1] // HEAD_DIM
    head_each = heads == count

    reach = BAND_REACH if rows * count == 1024 else rows * count

    if head_each:
        attn_packed = attn_pack(attn_query, attn_key, attn_value, attn_output, attn_grad_out)
        attn_in = lax.all_to_all(attn_packed, DEVICES, split_axis=0, concat_axis=0, tiled=True)

    packed = conv_pack(conv_query, conv_key, conv_value, conv_grad_out, inner, ch_count)
    pieces = [packed[0]] + [exchanged(packed[k], k, count) for k in range(1, members)]
    group_count = channels // members // GROUP
    y = lax.rem(lax.axis_index("seq"), inner)
    taps = lax.dynamic_slice_in_dim(conv_filter, y * group_count, group_count, 0).astype(F32)
    rev_taps = jnp.roll(taps[:, ::-1], 1, axis=1)
    taps, rev_taps, *pieces = lax.optimization_barrier((taps, rev_taps, *pieces))
    mixed_lo, mixed_hi, grad_lo, grad_hi = conv_join(pieces, rows, inner, ch_count)
    if head_each:
        attn_in, mixed_hi, grad_lo = lax.optimization_barrier((attn_in, mixed_hi, grad_lo))
    prior, later = shifted(mixed_hi, members, count), shifted(grad_lo, -members, count)
    if head_each:
        attn_back = attn_head(doc_lengths, attn_in, rows, reach)
        attn_back, taps, rev_taps = lax.optimization_barrier((attn_back, taps, rev_taps))
        attn_res = lax.all_to_all(attn_back, DEVICES, split_axis=0, concat_axis=0, tiled=True)
    own = (prior, mixed_lo, mixed_hi, grad_lo, grad_hi, later)
    filter_part = conv_filter_grad(doc_lengths, own[:5], rows, inner, ch_count)
    other = exchanged(filter_part, members, count)
    taps, filter_part = lax.optimization_barrier((taps, filter_part))
    conv_back = conv_core(doc_lengths, taps, rev_taps, own, rows, inner, ch_count)
    conv_res = [conv_back[0]] + [exchanged(conv_back[k], k, count) for k in range(1, members)]
    filter_part, other, conv_res[1:4] = lax.optimization_barrier(
        (filter_part, other, conv_res[1:4])
    )
    filter_part = filter_part + other
    distance = 2 * members
    while distance < count:
        other = exchanged(filter_part, distance, count)
        conv_res, other = lax.optimization_barrier((conv_res, other))
        filter_part = filter_part + other
        distance *= 2
    filter_part = jnp.roll(filter_part[:, ::-1], 1, axis=1)
    other = exchanged(filter_part, ch_count, count)
    grad_conv = conv_unpack(conv_res, conv_key, conv_value, conv_grad_out, inner, ch_count)
    other, *grad_conv = lax.optimization_barrier((other, *grad_conv))
    if head_each:
        *grad_attn, grad_filter = attn_unpack(attn_res, filter_part, other, rows, inner)
    else:
        grad_attn = attn_gathered(
            attn_query, attn_key, attn_value, attn_output, attn_grad_out, doc_lengths
        )
        grad_filter = jnp.where(
            y == 0,
            jnp.concatenate([filter_part, other], axis=0),
            jnp.concatenate([other, filter_part], axis=0),
        )
    return (*grad_attn, *grad_conv, grad_filter)


def solution(mesh):
    rows = P(("seq", "ch"), None)
    return jax.shard_map(
        body,
        mesh=mesh,
        in_specs=(rows,) * 9 + (P("ch", None), P()),
        out_specs=(rows,) * 6 + (P("ch", None),),
        check_vma=False,
    )
```

```python
import functools
import math

import jax
import jax.numpy as jnp
from jax import lax
from jax.experimental import pallas as pl
from jax.experimental.pallas import tpu as pltpu
from jax.sharding import PartitionSpec as P

HEAD_DIM = 128
GROUP = 16
FILTER_LEN = 128
LANES = 128
EACH = 2
BAND_REACH = 320
DEVICES = ("seq", "ch")
NEG_FILL = -1e30
BF16 = jnp.bfloat16
F32 = jnp.float32

NT = (((1,), (1,)), ((), ()))
NN = (((1,), (0,)), ((), ()))
TN = (((0,), (0,)), ((), ()))


def dot(a, b, dims):
    return lax.dot_general(a, b, dims, preferred_element_type=F32)


def params():
    return pltpu.CompilerParams(vmem_limit_bytes=40 * 1024 * 1024)


def cost(flops, bytes_accessed):
    return pl.CostEstimate(flops=flops, bytes_accessed=bytes_accessed, transcendentals=0)


def split_terms(x):
    high = x.astype(BF16)
    low = (x - high.astype(F32)).astype(BF16)
    return high, low


def doc_start(lens_ref, positions):
    start = jnp.zeros_like(positions)
    end = jnp.int32(0)
    for d in range(lens_ref.shape[0]):
        end = end + lens_ref[d]
        start = jnp.where(positions >= end, end, start)
    return start


def member_index(ch_count, inner):
    return lax.rem(lax.axis_index("seq"), inner) * ch_count + lax.axis_index("ch")


def chunk_piece(chunk, ch_count, inner):
    owner = lax.rem(chunk, inner) * ch_count + chunk // inner
    return jnp.bitwise_xor(owner, member_index(ch_count, inner))


def conv_pack_kernel(inner, ch_count, cq_ref, ck_ref, cv_ref, cg_ref, *out_refs):
    rows = cq_ref.shape[0]
    piece = chunk_piece(pl.program_id(0), ch_count, inner)
    mixed = (ck_ref[...].astype(F32) * cv_ref[...].astype(F32)).astype(BF16)
    grad = (cg_ref[...].astype(F32) * cq_ref[...].astype(F32)).astype(BF16)
    for k, out_ref in enumerate(out_refs):

        @pl.when(piece == k)
        def _():
            out_ref[0:rows, :] = mixed
            out_ref[rows:, :] = grad


def conv_pack(cq, ck, cv, cg, inner, ch_count):
    rows, channels = cq.shape
    members = inner * ch_count
    width = channels // members
    spec = pl.BlockSpec((rows, width), lambda k: (0, k))
    return pl.pallas_call(
        functools.partial(conv_pack_kernel, inner, ch_count),
        grid=(members,),
        in_specs=[spec] * 4,
        out_specs=[pl.BlockSpec((2 * rows, width), lambda k: (0, 0))] * members,
        out_shape=[jax.ShapeDtypeStruct((2 * rows, width), BF16)] * members,
        cost_estimate=cost(4 * rows * channels, 12 * rows * channels),
        compiler_params=params(),
        name="conv_pack",
    )(cq, ck, cv, cg)


def conv_join_kernel(rows, inner, ch_count, *refs):
    members = inner * ch_count
    pieces, outs = refs[:members], refs[members:]
    half = members // 2
    me = member_index(ch_count, inner)
    for k, x_ref in enumerate(pieces):
        source = jnp.bitwise_xor(me, k)
        for part in range(2):

            @pl.when(source // half == part)
            def _():
                at = pl.multiple_of((source - part * half) * rows, rows)
                outs[part][pl.ds(at, rows), :] = x_ref[0:rows, :]
                outs[2 + part][pl.ds(at, rows), :] = x_ref[rows : 2 * rows, :]


def conv_join(pieces, rows, inner, ch_count):
    members, width = len(pieces), pieces[0].shape[1]
    step = min(width, 512)
    shape = jax.ShapeDtypeStruct((members * rows // 2, width), BF16)
    return pl.pallas_call(
        functools.partial(conv_join_kernel, rows, inner, ch_count),
        grid=(width // step,),
        in_specs=[pl.BlockSpec((2 * rows, step), lambda j: (0, j))] * members,
        out_specs=[pl.BlockSpec((members * rows // 2, step), lambda j: (0, j))] * 4,
        out_shape=[shape] * 4,
        cost_estimate=cost(0, 8 * members * rows * width),
        name="conv_join",
    )(*pieces)


def attn_pack_kernel(rows, q_ref, k_ref, v_ref, o_ref, g_ref, out_ref):
    heads = q_ref.shape[1] // HEAD_DIM
    span = LANES // rows
    offset = lax.rem(lax.axis_index("ch"), span) * rows
    product = g_ref[...].astype(F32) * o_ref[...].astype(F32)
    shape = (max(heads, 8), heads * HEAD_DIM)
    owner = lax.broadcasted_iota(jnp.int32, shape, 1) // HEAD_DIM
    chosen = (owner == lax.broadcasted_iota(jnp.int32, shape, 0)).astype(F32).astype(BF16)
    high, low = split_terms(product)
    delta = dot(chosen, high, NT) + dot(chosen, low, NT)
    delta = jnp.concatenate([delta, jnp.zeros((delta.shape[0], LANES - rows), F32)], axis=1)
    delta = pltpu.roll(delta, offset, 1)
    high = delta.astype(BF16).astype(F32)
    low = delta - high
    row = lax.broadcasted_iota(jnp.int32, (16, LANES), 0)
    for h in range(heads):
        cols = slice(h * HEAD_DIM, (h + 1) * HEAD_DIM)
        out_ref[h, 0:rows, :] = q_ref[:, cols]
        out_ref[h, rows : 2 * rows, :] = k_ref[:, cols]
        out_ref[h, 2 * rows : 3 * rows, :] = v_ref[:, cols]
        out_ref[h, 3 * rows : 4 * rows, :] = g_ref[:, cols]
        tile = jnp.where(row == 0, high[h : h + 1], jnp.where(row == 1, low[h : h + 1], 0.0))
        out_ref[h, 4 * rows : 4 * rows + 16, :] = tile.astype(BF16)


def attn_pack(q, k, v, o, g):
    rows, features = q.shape
    heads = features // HEAD_DIM
    step = math.gcd(heads, 16)
    spec = pl.BlockSpec((rows, step * HEAD_DIM), lambda j: (0, j))
    height = 4 * rows + 16
    return pl.pallas_call(
        functools.partial(attn_pack_kernel, rows),
        grid=(heads // step,),
        in_specs=[spec] * 5,
        out_specs=pl.BlockSpec((step, height, HEAD_DIM), lambda j: (j, 0, 0)),
        out_shape=jax.ShapeDtypeStruct((heads, height, HEAD_DIM), BF16),
        cost_estimate=cost(4 * rows * features, 20 * rows * features),
        name="attn_pack",
    )(q, k, v, o, g)


def attn_kernel(rows, reach, lens_ref, x_ref, out_ref, dk_ref, dv_ref):
    sources = x_ref.shape[0]
    per = LANES // rows
    blocks = sources // per
    scale = 1.0 / math.sqrt(HEAD_DIM)

    def part(first, count, which):
        return x_ref[first * per : (first + count) * per, which * rows : (which + 1) * rows, :].reshape(
            count * LANES, HEAD_DIM
        )

    dk_ref[...] = jnp.zeros_like(dk_ref)
    dv_ref[...] = jnp.zeros_like(dv_ref)
    for i in range(blocks):
        low = max(0, (i * LANES - (reach - 1)) // LANES)
        count = i + 1 - low
        query, grad = part(i, 1, 0), part(i, 1, 3)
        keys, values = part(low, count, 1), part(low, count, 2)
        delta = x_ref[i * per : (i + 1) * per, 4 * rows : 4 * rows + 16, :].astype(F32)
        delta = jnp.sum(jnp.sum(delta, axis=0), axis=0, keepdims=True)
        q_pos = i * LANES + lax.broadcasted_iota(jnp.int32, (8, LANES), 1)
        start = doc_start(lens_ref, q_pos)[0:1]
        k_pos = low * LANES + lax.broadcasted_iota(jnp.int32, (count * LANES, LANES), 0)
        visible = (k_pos >= start) & (k_pos <= q_pos[0:1])
        scores = jnp.where(visible, dot(keys, query, NT) * scale, NEG_FILL)
        top = jnp.max(scores, axis=0, keepdims=True)
        weights = jnp.where(visible, jnp.exp(scores - top), 0.0)
        probs = weights * (1.0 / jnp.sum(weights, axis=0, keepdims=True))
        grad_probs = dot(values, grad, NT)
        grad_scores = probs * (grad_probs - delta)
        span = slice(low * LANES, (i + 1) * LANES)
        p_terms = jnp.concatenate(split_terms(probs), axis=1)
        dv_ref[span, :] += dot(p_terms, jnp.concatenate([grad, grad], axis=0), NN)
        s_high, s_low = split_terms(grad_scores)
        s_terms = jnp.concatenate([s_high, s_low], axis=1)
        dk_ref[span, :] += dot(s_terms, jnp.concatenate([query, query], axis=0), NN)
        dq = dot(s_high, keys, TN) + dot(s_low, keys, TN)
        out_ref[i * per : (i + 1) * per, 0:rows, :] = (
            (dq * scale).astype(BF16).reshape(per, rows, HEAD_DIM)
        )
    for i in range(blocks):
        span = slice(i * LANES, (i + 1) * LANES)
        here = slice(i * per, (i + 1) * per)
        out_ref[here, rows : 2 * rows, :] = (
            (dk_ref[span, :] * scale).astype(BF16).reshape(per, rows, HEAD_DIM)
        )
        out_ref[here, 2 * rows : 3 * rows, :] = (
            dv_ref[span, :].astype(BF16).reshape(per, rows, HEAD_DIM)
        )


def attn_head(lens, x, rows, reach):
    sources = x.shape[0]
    tokens = sources * rows
    return pl.pallas_call(
        functools.partial(attn_kernel, rows, reach),
        in_specs=[
            pl.BlockSpec(memory_space=pltpu.SMEM),
            pl.BlockSpec(memory_space=pltpu.VMEM),
        ],
        out_specs=pl.BlockSpec(memory_space=pltpu.VMEM),
        out_shape=jax.ShapeDtypeStruct((sources, 3 * rows, HEAD_DIM), BF16),
        scratch_shapes=[
            pltpu.VMEM((tokens, HEAD_DIM), F32),
            pltpu.VMEM((tokens, HEAD_DIM), F32),
        ],
        cost_estimate=cost(tokens, x.size),
        compiler_params=pltpu.CompilerParams(vmem_limit_bytes=40 * 1024 * 1024),
        name="attn_head",
    )(lens, x)


def attn_unpack_kernel(rows, inner, x_ref, mine_ref, other_ref, dq_ref, dk_ref, dv_ref, filt_ref):
    for h in range(x_ref.shape[0]):
        cols = slice(h * HEAD_DIM, (h + 1) * HEAD_DIM)
        dq_ref[:, cols] = x_ref[h, 0:rows, :]
        dk_ref[:, cols] = x_ref[h, rows : 2 * rows, :]
        dv_ref[:, cols] = x_ref[h, 2 * rows : 3 * rows, :]

    @pl.when(pl.program_id(0) == 0)
    def _():
        groups = mine_ref.shape[0]
        at = lax.rem(lax.axis_index("seq"), inner) * groups
        filt_ref[pl.ds(pl.multiple_of(at, groups), groups), :] = mine_ref[...]
        at = groups - at
        filt_ref[pl.ds(pl.multiple_of(at, groups), groups), :] = other_ref[...]


def attn_unpack(x, mine, other, rows, inner):
    heads = x.shape[0]
    step = math.gcd(heads, 16)
    spec = pl.BlockSpec((rows, step * HEAD_DIM), lambda j: (0, j))
    half = pl.BlockSpec(mine.shape, lambda j: (0, 0))
    whole = (2 * mine.shape[0], mine.shape[1])
    shape = jax.ShapeDtypeStruct((rows, heads * HEAD_DIM), BF16)
    return pl.pallas_call(
        functools.partial(attn_unpack_kernel, rows, inner),
        grid=(heads // step,),
        in_specs=[pl.BlockSpec((step, 3 * rows, HEAD_DIM), lambda j: (j, 0, 0)), half, half],
        out_specs=[spec] * 3 + [pl.BlockSpec(whole, lambda j: (0, 0))],
        out_shape=[shape] * 3 + [jax.ShapeDtypeStruct(whole, F32)],
        compiler_params=params(),
        cost_estimate=cost(0, 4 * x.size),
        name="attn_unpack",
    )(x, mine, other)


def circulant(row):
    rolled = pltpu.roll(jnp.broadcast_to(row, (8, LANES)), 0, 1, stride=1, stride_axis=0)
    pieces = [rolled if a == 0 else pltpu.roll(rolled, 8 * a, 1) for a in range(LANES // 8)]
    full = jnp.concatenate(pieces, axis=0).astype(BF16)
    return jnp.concatenate([full, full], axis=1)


def unskewed(outer):
    sub = lax.broadcasted_iota(jnp.int32, (8, LANES), 0)
    folded = outer[0:8]
    for a in range(1, LANES // 8):
        folded = folded + pltpu.roll(outer[8 * a : 8 * a + 8], LANES - 8 * a, 1)
    for bit in (1, 2, 4):
        folded = jnp.where((sub & bit) != 0, pltpu.roll(folded, LANES - bit, 1), folded)
    return jnp.sum(folded, axis=0, keepdims=True)


def reached(lens_ref, out_pos, in_pos):
    gap = out_pos - in_pos
    near = (gap >= 0) & (gap < FILTER_LEN) & (in_pos >= doc_start(lens_ref, out_pos))
    return near.astype(F32).astype(BF16)


def window_positions(inner, span):
    base = (lax.axis_index("seq") // inner) * span
    shape = (LANES, 2 * LANES)
    return (
        base + lax.broadcasted_iota(jnp.int32, shape, 0),
        base + lax.broadcasted_iota(jnp.int32, shape, 1),
    )


def conv_core_kernel(
    rows, inner, ch_count, lens_ref, tap_ref, rev_ref, prior_ref, m0_ref, m1_ref, g0_ref, g1_ref,
    later_ref, *refs,
):
    members = inner * ch_count
    outs = refs[:members]
    conv_ref, down_ref = refs[members:]
    me = member_index(ch_count, inner)
    groups = LANES // GROUP
    blocks = 2
    down, across = window_positions(inner, members * rows)
    back = [reached(lens_ref, down + b * LANES, across + (b - 1) * LANES) for b in range(blocks)]
    front = [reached(lens_ref, across + b * LANES, down + b * LANES) for b in range(blocks)]

    for tile in range(m0_ref.shape[1] // LANES):
        cols = slice(tile * LANES, (tile + 1) * LANES)
        mixed = [r[:, cols] for r in (prior_ref, m0_ref, m1_ref)]
        grad = [r[:, cols] for r in (g0_ref, g1_ref, later_ref)]
        lane_group = lax.broadcasted_iota(jnp.int32, (LANES, LANES), 1) // GROUP
        tap_rows = slice(tile * groups, (tile + 1) * groups)
        taps, rev_taps = tap_ref[tap_rows, :], rev_ref[tap_rows, :]
        back_taps = [circulant(rev_taps[g : g + 1]) for g in range(groups)]
        front_taps = [circulant(taps[g : g + 1]) for g in range(groups)]
        for b in range(blocks):
            window = jnp.concatenate(mixed[b : b + 2], axis=0)
            ahead = jnp.concatenate(grad[b : b + 2], axis=0)
            conv_all = dot(jnp.concatenate([t * back[b] for t in back_taps], axis=0), window, NN)
            down_all = dot(jnp.concatenate([t * front[b] for t in front_taps], axis=0), ahead, NN)
            conv_out = jnp.zeros((LANES, LANES), F32)
            mixed_grad = jnp.zeros((LANES, LANES), F32)
            for g in range(groups):
                mine = lane_group == g
                span = slice(g * LANES, (g + 1) * LANES)
                conv_out = jnp.where(mine, conv_all[span], conv_out)
                mixed_grad = jnp.where(mine, down_all[span], mixed_grad)
            here = slice(b * LANES, (b + 1) * LANES)
            conv_ref[here, cols] = conv_out.astype(BF16)
            down_ref[here, cols] = mixed_grad.astype(BF16)
    for k, out_ref in enumerate(outs):
        at = pl.multiple_of(jnp.bitwise_xor(me, k) * rows, rows)
        out_ref[0:rows, :] = conv_ref[pl.ds(at, rows), :]
        out_ref[rows : 2 * rows, :] = down_ref[pl.ds(at, rows), :]


def conv_core(lens, taps, rev_taps, arrays, rows, inner, ch_count):
    members = inner * ch_count
    width = arrays[0].shape[1]
    vmem = pl.BlockSpec(memory_space=pltpu.VMEM)
    return pl.pallas_call(
        functools.partial(conv_core_kernel, rows, inner, ch_count),
        in_specs=[pl.BlockSpec(memory_space=pltpu.SMEM)] + [vmem] * 8,
        out_specs=[vmem] * members,
        out_shape=[jax.ShapeDtypeStruct((2 * rows, width), BF16)] * members,
        scratch_shapes=[pltpu.VMEM((2 * LANES, width), BF16)] * 2,
        cost_estimate=cost(2000 * LANES * LANES * width, 24 * LANES * width),
        compiler_params=pltpu.CompilerParams(vmem_limit_bytes=40 * 1024 * 1024),
        name="conv_core",
    )(lens, taps, rev_taps, *arrays)


def conv_filter_kernel(
    rows, inner, ch_count, lens_ref, prior_ref, m0_ref, m1_ref, g0_ref, g1_ref, filt_ref
):
    groups = LANES // GROUP
    blocks = 2
    down, across = window_positions(inner, inner * ch_count * rows)
    back = [
        reached(lens_ref, down + b * LANES, across + (b - 1) * LANES).astype(F32)
        for b in range(blocks)
    ]
    for tile in range(m0_ref.shape[1] // LANES):
        cols = slice(tile * LANES, (tile + 1) * LANES)
        mixed = [r[:, cols] for r in (prior_ref, m0_ref, m1_ref)]
        grad = [r[:, cols] for r in (g0_ref, g1_ref)]
        lane_group = lax.broadcasted_iota(jnp.int32, (LANES, LANES), 1) // GROUP
        sums = []
        for g in range(groups):
            mine = (lane_group == g).astype(F32).astype(BF16)
            outer = jnp.zeros((LANES, LANES), F32)
            for b in range(blocks):
                window = jnp.concatenate(mixed[b : b + 2], axis=0)
                full = dot(grad[b] * mine, window, NT) * back[b]
                outer = outer + full[:, 0:LANES] + full[:, LANES:]
            sums.append(unskewed(outer))
        filt_ref[tile * groups : (tile + 1) * groups, :] = jnp.concatenate(sums, axis=0)


def conv_filter_grad(lens, arrays, rows, inner, ch_count):
    width = arrays[0].shape[1]
    vmem = pl.BlockSpec(memory_space=pltpu.VMEM)
    return pl.pallas_call(
        functools.partial(conv_filter_kernel, rows, inner, ch_count),
        in_specs=[pl.BlockSpec(memory_space=pltpu.SMEM)] + [vmem] * 5,
        out_specs=vmem,
        out_shape=jax.ShapeDtypeStruct((width // GROUP, FILTER_LEN), F32),
        cost_estimate=cost(32 * LANES * LANES * width, 10 * LANES * width),
        compiler_params=pltpu.CompilerParams(vmem_limit_bytes=40 * 1024 * 1024),
        name="conv_filter_grad",
    )(lens, *arrays)


def conv_unpack_kernel(inner, ch_count, each, ck_ref, cv_ref, cg_ref, *refs):
    members = inner * ch_count
    pieces, (gq_ref, gk_ref, gv_ref) = refs[:members], refs[members:]
    rows, width = pieces[0].shape[0] // 2, pieces[0].shape[1]
    for part in range(each):
        piece = chunk_piece(pl.program_id(0) * each + part, ch_count, inner)
        cols = slice(part * width, (part + 1) * width)
        for k, x_ref in enumerate(pieces):

            @pl.when(piece == k)
            def _():
                conv_out = x_ref[0:rows, :].astype(F32)
                mixed_grad = x_ref[rows : 2 * rows, :].astype(F32)
                gq_ref[:, cols] = (cg_ref[:, cols].astype(F32) * conv_out).astype(BF16)
                gk_ref[:, cols] = (mixed_grad * cv_ref[:, cols].astype(F32)).astype(BF16)
                gv_ref[:, cols] = (mixed_grad * ck_ref[:, cols].astype(F32)).astype(BF16)


def conv_unpack(pieces, ck, cv, cg, inner, ch_count):
    rows, channels = ck.shape
    members = inner * ch_count
    each = EACH
    width = each * channels // members
    spec = pl.BlockSpec((rows, width), lambda k: (0, k))
    shape = jax.ShapeDtypeStruct((rows, channels), BF16)
    return pl.pallas_call(
        functools.partial(conv_unpack_kernel, inner, ch_count, each),
        grid=(members // each,),
        in_specs=[spec] * 3 + [pl.BlockSpec(pieces[0].shape, lambda k: (0, 0))] * members,
        out_specs=[spec] * 3,
        out_shape=[shape] * 3,
        compiler_params=params(),
        cost_estimate=cost(6 * rows * channels, 16 * rows * channels),
        name="conv_unpack",
    )(ck, cv, cg, *pieces)


def doc_index(doc_lengths, positions):
    doc_ends = jnp.cumsum(doc_lengths)
    return jnp.sum((doc_ends[None, :] <= positions[:, None]).astype(jnp.int32), axis=1)


def split_rows(advance, carried, pieces):
    def one_block(block_index, current):
        sub_parts = tuple(
            lax.dynamic_slice_in_dim(part, block_index * 512, 512, 0) for part in pieces
        )
        return advance(current, sub_parts, block_index * 512)

    return lax.fori_loop(0, pieces[0].shape[0] // 512, one_block, carried)


def attn_gathered(attn_query, attn_key, attn_value, attn_output, attn_grad_out, doc_lengths):
    query_rows, key_rows, value_rows, output_rows, grad_rows = (
        lax.all_to_all(a, "ch", split_axis=1, concat_axis=0, tiled=True)
        for a in (attn_query, attn_key, attn_value, attn_output, attn_grad_out)
    )
    tok_rows = query_rows.shape[0]
    head_count = query_rows.shape[1] // HEAD_DIM
    scale_factor = 1.0 / math.sqrt(HEAD_DIM)
    local_pos = lax.axis_index("seq") * tok_rows + jnp.arange(tok_rows, dtype=jnp.int32)
    local_doc = doc_index(doc_lengths, local_pos)
    query_heads, key_heads, value_heads, output_heads, grad_heads = (
        a.reshape(tok_rows, head_count, HEAD_DIM)
        for a in (query_rows, key_rows, value_rows, output_rows, grad_rows)
    )
    delta_rows = jnp.sum(grad_heads.astype(F32) * output_heads.astype(F32), axis=2)
    delta_heads = delta_rows.T

    def key_step(carried, pieces, key_start):
        key_part, value_part = pieces
        key_pos = key_start + jnp.arange(key_part.shape[0], dtype=jnp.int32)
        key_doc = doc_index(doc_lengths, key_pos)
        visible = (key_doc[None, :] == local_doc[:, None]) & (key_pos[None, :] <= local_pos[:, None])
        running_max, running_sum, running_grad = carried
        scores = (
            jnp.einsum("thd,rhd->htr", query_heads, key_part, preferred_element_type=F32)
            * scale_factor
        )
        new_max = jnp.maximum(
            running_max, jnp.max(jnp.where(visible[None], scores, NEG_FILL), axis=2)
        )
        weights = jnp.where(visible[None], jnp.exp(scores - new_max[:, :, None]), 0.0)
        rescale = jnp.exp(running_max - new_max)
        grad_probs = jnp.einsum(
            "thd,rhd->htr", grad_heads, value_part, preferred_element_type=F32
        )
        weighted = weights * (grad_probs - delta_heads[:, :, None])
        update = jnp.einsum(
            "htr,rhd->htd", weighted, key_part.astype(F32), precision=lax.Precision.HIGHEST
        )
        return (
            new_max,
            running_sum * rescale + jnp.sum(weights, axis=2),
            running_grad * rescale[:, :, None] + update,
        )

    start_state = (
        jnp.full((head_count, tok_rows), NEG_FILL, F32),
        jnp.zeros((head_count, tok_rows), F32),
        jnp.zeros((head_count, tok_rows, HEAD_DIM), F32),
    )
    final_max, final_sum, final_grad = split_rows(
        key_step,
        start_state,
        (
            lax.all_gather(key_heads, "seq", axis=0, tiled=True),
            lax.all_gather(value_heads, "seq", axis=0, tiled=True),
        ),
    )
    lse_rows = (final_max + jnp.log(final_sum)).T
    grad_query = (final_grad * (scale_factor / final_sum)[:, :, None]).transpose(1, 0, 2)
    lse_whole = lax.all_gather(lse_rows, "seq", axis=0, tiled=True)
    delta_whole = lax.all_gather(delta_rows, "seq", axis=0, tiled=True)

    def query_step(carried, pieces, query_start):
        query_part, grad_part = pieces
        part_rows = query_part.shape[0]
        lse_part = lax.dynamic_slice_in_dim(lse_whole, query_start, part_rows, 0)
        delta_part = lax.dynamic_slice_in_dim(delta_whole, query_start, part_rows, 0)
        query_pos = query_start + jnp.arange(part_rows, dtype=jnp.int32)
        query_doc = doc_index(doc_lengths, query_pos)
        visible = (query_doc[:, None] == local_doc[None, :]) & (
            local_pos[None, :] <= query_pos[:, None]
        )
        key_grad, value_grad = carried
        scores = (
            jnp.einsum("rhd,thd->hrt", query_part, key_heads, preferred_element_type=F32)
            * scale_factor
        )
        probs = jnp.where(visible[None], jnp.exp(scores - lse_part.T[:, :, None]), 0.0)
        value_grad = value_grad + jnp.einsum(
            "hrt,rhd->thd", probs, grad_part.astype(F32), precision=lax.Precision.HIGHEST
        )
        grad_probs = jnp.einsum(
            "rhd,thd->hrt", grad_part, value_heads, preferred_element_type=F32
        )
        grad_scores = probs * (grad_probs - delta_part.T[:, :, None])
        key_grad = key_grad + scale_factor * jnp.einsum(
            "hrt,rhd->thd", grad_scores, query_part.astype(F32), precision=lax.Precision.HIGHEST
        )
        return (key_grad, value_grad)

    zero = jnp.zeros((tok_rows, head_count, HEAD_DIM), F32)
    key_grad, value_grad = split_rows(
        query_step,
        (zero, zero),
        (
            lax.all_gather(query_heads, "seq", axis=0, tiled=True),
            lax.all_gather(grad_heads, "seq", axis=0, tiled=True),
        ),
    )
    return tuple(
        lax.all_to_all(
            a.reshape(tok_rows, head_count * HEAD_DIM).astype(BF16),
            "ch",
            split_axis=0,
            concat_axis=1,
            tiled=True,
        )
        for a in (grad_query, key_grad, value_grad)
    )


def shifted(block, distance, count):
    route = [(i, i + distance) for i in range(count) if 0 <= i + distance < count]
    return lax.ppermute(block, DEVICES, route)


def exchanged(block, distance, count):
    return lax.ppermute(block, DEVICES, [(i, i ^ distance) for i in range(count)])


def body(
    attn_query, attn_key, attn_value, attn_output, attn_grad_out,
    conv_query, conv_key, conv_value, conv_grad_out, conv_filter, doc_lengths,
):
    seq_count, ch_count = lax.axis_size("seq"), lax.axis_size("ch")
    count = seq_count * ch_count
    rows, channels = conv_query.shape
    inner = 2
    members = inner * ch_count
    outer = seq_count // inner
    heads = attn_query.shape[1] // HEAD_DIM
    head_each = heads == count

    reach = BAND_REACH if rows * count == 1024 else rows * count

    if head_each:
        attn_packed = attn_pack(attn_query, attn_key, attn_value, attn_output, attn_grad_out)
        attn_in = lax.all_to_all(attn_packed, DEVICES, split_axis=0, concat_axis=0, tiled=True)

    packed = conv_pack(conv_query, conv_key, conv_value, conv_grad_out, inner, ch_count)
    packed = list(packed)
    pieces = [packed[0], exchanged(packed[1], 1, count)]
    packed[-1], pieces[1] = lax.optimization_barrier((packed[-1], pieces[1]))
    pieces += [exchanged(packed[k], k, count) for k in range(2, members)]
    group_count = channels // members // GROUP
    y = lax.rem(lax.axis_index("seq"), inner)
    taps = lax.dynamic_slice_in_dim(conv_filter, y * group_count, group_count, 0).astype(F32)
    rev_taps = jnp.roll(taps[:, ::-1], 1, axis=1)
    taps, rev_taps, *pieces = lax.optimization_barrier((taps, rev_taps, *pieces))
    mixed_lo, mixed_hi, grad_lo, grad_hi = conv_join(pieces, rows, inner, ch_count)
    if head_each:
        attn_in, mixed_hi, grad_lo = lax.optimization_barrier((attn_in, mixed_hi, grad_lo))
    prior, later = shifted(mixed_hi, members, count), shifted(grad_lo, -members, count)
    if head_each:
        attn_back = attn_head(doc_lengths, attn_in, rows, reach)
        attn_back, taps, rev_taps = lax.optimization_barrier((attn_back, taps, rev_taps))
        attn_res = lax.all_to_all(attn_back, DEVICES, split_axis=0, concat_axis=0, tiled=True)
    own = (prior, mixed_lo, mixed_hi, grad_lo, grad_hi, later)
    filter_part = conv_filter_grad(doc_lengths, own[:5], rows, inner, ch_count)
    other = exchanged(filter_part, members, count)
    taps, filter_part = lax.optimization_barrier((taps, filter_part))
    conv_back = conv_core(doc_lengths, taps, rev_taps, own, rows, inner, ch_count)
    conv_back = list(conv_back)
    conv_res = [conv_back[0], exchanged(conv_back[1], 1, count)]
    conv_back[-1], conv_res[1] = lax.optimization_barrier((conv_back[-1], conv_res[1]))
    conv_res += [exchanged(conv_back[k], k, count) for k in range(2, members)]
    filter_part, other, conv_res[1:4] = lax.optimization_barrier(
        (filter_part, other, conv_res[1:4])
    )
    filter_part = filter_part + other
    distance = 2 * members
    while distance < count:
        other = exchanged(filter_part, distance, count)
        conv_res, other = lax.optimization_barrier((conv_res, other))
        filter_part = filter_part + other
        distance *= 2
    filter_part = jnp.roll(filter_part[:, ::-1], 1, axis=1)
    other = exchanged(filter_part, ch_count, count)
    grad_conv = conv_unpack(conv_res, conv_key, conv_value, conv_grad_out, inner, ch_count)
    other, *grad_conv = lax.optimization_barrier((other, *grad_conv))
    if head_each:
        *grad_attn, grad_filter = attn_unpack(attn_res, filter_part, other, rows, inner)
    else:
        grad_attn = attn_gathered(
            attn_query, attn_key, attn_value, attn_output, attn_grad_out, doc_lengths
        )
        grad_filter = jnp.where(
            y == 0,
            jnp.concatenate([filter_part, other], axis=0),
            jnp.concatenate([other, filter_part], axis=0),
        )
    return (*grad_attn, *grad_conv, grad_filter)


def solution(mesh):
    rows = P(("seq", "ch"), None)
    return jax.shard_map(
        body,
        mesh=mesh,
        in_specs=(rows,) * 9 + (P("ch", None), P()),
        out_specs=(rows,) * 6 + (P("ch", None),),
        check_vma=False,
    )
```

```python
import functools
import math

import jax
import jax.numpy as jnp
from jax import lax
from jax.experimental import pallas as pl
from jax.experimental.pallas import tpu as pltpu
from jax.sharding import PartitionSpec as P

HEAD_DIM = 128
GROUP = 16
FILTER_LEN = 128
LANES = 128
EACH = 2
BAND_REACH = 320
DEVICES = ("seq", "ch")
NEG_FILL = -1e30
BF16 = jnp.bfloat16
F32 = jnp.float32

NT = (((1,), (1,)), ((), ()))
NN = (((1,), (0,)), ((), ()))
TN = (((0,), (0,)), ((), ()))


def dot(a, b, dims):
    return lax.dot_general(a, b, dims, preferred_element_type=F32)


def params():
    return pltpu.CompilerParams(vmem_limit_bytes=40 * 1024 * 1024)


def cost(flops, bytes_accessed):
    return pl.CostEstimate(flops=flops, bytes_accessed=bytes_accessed, transcendentals=0)


def split_terms(x):
    high = x.astype(BF16)
    low = (x - high.astype(F32)).astype(BF16)
    return high, low


def doc_start(lens_ref, positions):
    start = jnp.zeros_like(positions)
    end = jnp.int32(0)
    for d in range(lens_ref.shape[0]):
        end = end + lens_ref[d]
        start = jnp.where(positions >= end, end, start)
    return start


def member_index(ch_count, inner):
    return lax.rem(lax.axis_index("seq"), inner) * ch_count + lax.axis_index("ch")


def chunk_piece(chunk, ch_count, inner):
    owner = lax.rem(chunk, inner) * ch_count + chunk // inner
    return jnp.bitwise_xor(owner, member_index(ch_count, inner))


def conv_pack_kernel(inner, ch_count, cq_ref, ck_ref, cv_ref, cg_ref, *out_refs):
    rows = cq_ref.shape[0]
    piece = chunk_piece(pl.program_id(0), ch_count, inner)
    mixed = (ck_ref[...].astype(F32) * cv_ref[...].astype(F32)).astype(BF16)
    grad = (cg_ref[...].astype(F32) * cq_ref[...].astype(F32)).astype(BF16)
    for k, out_ref in enumerate(out_refs):

        @pl.when(piece == k)
        def _():
            out_ref[0:rows, :] = mixed
            out_ref[rows:, :] = grad


def conv_pack(cq, ck, cv, cg, inner, ch_count):
    rows, channels = cq.shape
    members = inner * ch_count
    width = channels // members
    spec = pl.BlockSpec((rows, width), lambda k: (0, k))
    return pl.pallas_call(
        functools.partial(conv_pack_kernel, inner, ch_count),
        grid=(members,),
        in_specs=[spec] * 4,
        out_specs=[pl.BlockSpec((2 * rows, width), lambda k: (0, 0))] * members,
        out_shape=[jax.ShapeDtypeStruct((2 * rows, width), BF16)] * members,
        cost_estimate=cost(4 * rows * channels, 12 * rows * channels),
        compiler_params=params(),
        name="conv_pack",
    )(cq, ck, cv, cg)


def conv_join_kernel(rows, inner, ch_count, *refs):
    members = inner * ch_count
    pieces, outs = refs[:members], refs[members:]
    half = members // 2
    me = member_index(ch_count, inner)
    for k, x_ref in enumerate(pieces):
        source = jnp.bitwise_xor(me, k)
        for part in range(2):

            @pl.when(source // half == part)
            def _():
                at = pl.multiple_of((source - part * half) * rows, rows)
                outs[part][pl.ds(at, rows), :] = x_ref[0:rows, :]
                outs[2 + part][pl.ds(at, rows), :] = x_ref[rows : 2 * rows, :]


def conv_join(pieces, rows, inner, ch_count):
    members, width = len(pieces), pieces[0].shape[1]
    step = min(width, 512)
    shape = jax.ShapeDtypeStruct((members * rows // 2, width), BF16)
    return pl.pallas_call(
        functools.partial(conv_join_kernel, rows, inner, ch_count),
        grid=(width // step,),
        in_specs=[pl.BlockSpec((2 * rows, step), lambda j: (0, j))] * members,
        out_specs=[pl.BlockSpec((members * rows // 2, step), lambda j: (0, j))] * 4,
        out_shape=[shape] * 4,
        cost_estimate=cost(0, 8 * members * rows * width),
        name="conv_join",
    )(*pieces)


def attn_pack_kernel(rows, q_ref, k_ref, v_ref, o_ref, g_ref, out_ref):
    heads = q_ref.shape[1] // HEAD_DIM
    span = LANES // rows
    offset = lax.rem(lax.axis_index("ch"), span) * rows
    product = g_ref[...].astype(F32) * o_ref[...].astype(F32)
    shape = (max(heads, 8), heads * HEAD_DIM)
    owner = lax.broadcasted_iota(jnp.int32, shape, 1) // HEAD_DIM
    chosen = (owner == lax.broadcasted_iota(jnp.int32, shape, 0)).astype(F32).astype(BF16)
    high, low = split_terms(product)
    delta = dot(chosen, high, NT) + dot(chosen, low, NT)
    delta = jnp.concatenate([delta, jnp.zeros((delta.shape[0], LANES - rows), F32)], axis=1)
    delta = pltpu.roll(delta, offset, 1)
    high = delta.astype(BF16).astype(F32)
    low = delta - high
    row = lax.broadcasted_iota(jnp.int32, (16, LANES), 0)
    for h in range(heads):
        cols = slice(h * HEAD_DIM, (h + 1) * HEAD_DIM)
        out_ref[h, 0:rows, :] = q_ref[:, cols]
        out_ref[h, rows : 2 * rows, :] = k_ref[:, cols]
        out_ref[h, 2 * rows : 3 * rows, :] = v_ref[:, cols]
        out_ref[h, 3 * rows : 4 * rows, :] = g_ref[:, cols]
        tile = jnp.where(row == 0, high[h : h + 1], jnp.where(row == 1, low[h : h + 1], 0.0))
        out_ref[h, 4 * rows : 4 * rows + 16, :] = tile.astype(BF16)


def attn_pack(q, k, v, o, g):
    rows, features = q.shape
    heads = features // HEAD_DIM
    step = math.gcd(heads, 16)
    spec = pl.BlockSpec((rows, step * HEAD_DIM), lambda j: (0, j))
    height = 4 * rows + 16
    return pl.pallas_call(
        functools.partial(attn_pack_kernel, rows),
        grid=(heads // step,),
        in_specs=[spec] * 5,
        out_specs=pl.BlockSpec((step, height, HEAD_DIM), lambda j: (j, 0, 0)),
        out_shape=jax.ShapeDtypeStruct((heads, height, HEAD_DIM), BF16),
        cost_estimate=cost(4 * rows * features, 20 * rows * features),
        name="attn_pack",
    )(q, k, v, o, g)


def attn_kernel(rows, reach, lens_ref, x_ref, out_ref, dk_ref, dv_ref):
    sources = x_ref.shape[0]
    per = LANES // rows
    blocks = sources // per
    scale = 1.0 / math.sqrt(HEAD_DIM)

    def part(first, count, which):
        return x_ref[first * per : (first + count) * per, which * rows : (which + 1) * rows, :].reshape(
            count * LANES, HEAD_DIM
        )

    dk_ref[...] = jnp.zeros_like(dk_ref)
    dv_ref[...] = jnp.zeros_like(dv_ref)
    for i in range(blocks):
        low = max(0, (i * LANES - (reach - 1)) // LANES)
        count = i + 1 - low
        query, grad = part(i, 1, 0), part(i, 1, 3)
        keys, values = part(low, count, 1), part(low, count, 2)
        delta = x_ref[i * per : (i + 1) * per, 4 * rows : 4 * rows + 16, :].astype(F32)
        delta = jnp.sum(jnp.sum(delta, axis=0), axis=0, keepdims=True)
        q_pos = i * LANES + lax.broadcasted_iota(jnp.int32, (8, LANES), 1)
        start = doc_start(lens_ref, q_pos)[0:1]
        k_pos = low * LANES + lax.broadcasted_iota(jnp.int32, (count * LANES, LANES), 0)
        visible = (k_pos >= start) & (k_pos <= q_pos[0:1])
        scores = jnp.where(visible, dot(keys, query, NT) * scale, NEG_FILL)
        top = jnp.max(scores, axis=0, keepdims=True)
        weights = jnp.exp(scores - top)
        probs = weights * (1.0 / jnp.sum(weights, axis=0, keepdims=True))
        grad_probs = dot(values, grad, NT)
        grad_scores = probs * (grad_probs - delta)
        span = slice(low * LANES, (i + 1) * LANES)
        p_terms = jnp.concatenate(split_terms(probs), axis=1)
        dv_ref[span, :] += dot(p_terms, jnp.concatenate([grad, grad], axis=0), NN)
        s_high, s_low = split_terms(grad_scores)
        s_terms = jnp.concatenate([s_high, s_low], axis=1)
        dk_ref[span, :] += dot(s_terms, jnp.concatenate([query, query], axis=0), NN)
        dq = dot(s_high, keys, TN) + dot(s_low, keys, TN)
        out_ref[i * per : (i + 1) * per, 0:rows, :] = (
            (dq * scale).astype(BF16).reshape(per, rows, HEAD_DIM)
        )
    for i in range(blocks):
        span = slice(i * LANES, (i + 1) * LANES)
        here = slice(i * per, (i + 1) * per)
        out_ref[here, rows : 2 * rows, :] = (
            (dk_ref[span, :] * scale).astype(BF16).reshape(per, rows, HEAD_DIM)
        )
        out_ref[here, 2 * rows : 3 * rows, :] = (
            dv_ref[span, :].astype(BF16).reshape(per, rows, HEAD_DIM)
        )


def attn_head(lens, x, rows, reach):
    sources = x.shape[0]
    tokens = sources * rows
    return pl.pallas_call(
        functools.partial(attn_kernel, rows, reach),
        in_specs=[
            pl.BlockSpec(memory_space=pltpu.SMEM),
            pl.BlockSpec(memory_space=pltpu.VMEM),
        ],
        out_specs=pl.BlockSpec(memory_space=pltpu.VMEM),
        out_shape=jax.ShapeDtypeStruct((sources, 3 * rows, HEAD_DIM), BF16),
        scratch_shapes=[
            pltpu.VMEM((tokens, HEAD_DIM), F32),
            pltpu.VMEM((tokens, HEAD_DIM), F32),
        ],
        cost_estimate=cost(tokens, x.size),
        compiler_params=pltpu.CompilerParams(vmem_limit_bytes=40 * 1024 * 1024),
        name="attn_head",
    )(lens, x)


def attn_unpack_kernel(rows, inner, x_ref, mine_ref, other_ref, dq_ref, dk_ref, dv_ref, filt_ref):
    for h in range(x_ref.shape[0]):
        cols = slice(h * HEAD_DIM, (h + 1) * HEAD_DIM)
        dq_ref[:, cols] = x_ref[h, 0:rows, :]
        dk_ref[:, cols] = x_ref[h, rows : 2 * rows, :]
        dv_ref[:, cols] = x_ref[h, 2 * rows : 3 * rows, :]

    @pl.when(pl.program_id(0) == 0)
    def _():
        groups = mine_ref.shape[0]
        at = lax.rem(lax.axis_index("seq"), inner) * groups
        filt_ref[pl.ds(pl.multiple_of(at, groups), groups), :] = mine_ref[...]
        at = groups - at
        filt_ref[pl.ds(pl.multiple_of(at, groups), groups), :] = other_ref[...]


def attn_unpack(x, mine, other, rows, inner):
    heads = x.shape[0]
    step = math.gcd(heads, 16)
    spec = pl.BlockSpec((rows, step * HEAD_DIM), lambda j: (0, j))
    half = pl.BlockSpec(mine.shape, lambda j: (0, 0))
    whole = (2 * mine.shape[0], mine.shape[1])
    shape = jax.ShapeDtypeStruct((rows, heads * HEAD_DIM), BF16)
    return pl.pallas_call(
        functools.partial(attn_unpack_kernel, rows, inner),
        grid=(heads // step,),
        in_specs=[pl.BlockSpec((step, 3 * rows, HEAD_DIM), lambda j: (j, 0, 0)), half, half],
        out_specs=[spec] * 3 + [pl.BlockSpec(whole, lambda j: (0, 0))],
        out_shape=[shape] * 3 + [jax.ShapeDtypeStruct(whole, F32)],
        compiler_params=params(),
        cost_estimate=cost(0, 4 * x.size),
        name="attn_unpack",
    )(x, mine, other)


def circulant(row):
    rolled = pltpu.roll(jnp.broadcast_to(row, (8, LANES)), 0, 1, stride=1, stride_axis=0)
    pieces = [rolled if a == 0 else pltpu.roll(rolled, 8 * a, 1) for a in range(LANES // 8)]
    full = jnp.concatenate(pieces, axis=0).astype(BF16)
    return jnp.concatenate([full, full], axis=1)


def unskewed(outer):
    sub = lax.broadcasted_iota(jnp.int32, (8, LANES), 0)
    folded = outer[0:8]
    for a in range(1, LANES // 8):
        folded = folded + pltpu.roll(outer[8 * a : 8 * a + 8], LANES - 8 * a, 1)
    for bit in (1, 2, 4):
        folded = jnp.where((sub & bit) != 0, pltpu.roll(folded, LANES - bit, 1), folded)
    return jnp.sum(folded, axis=0, keepdims=True)


def reached(lens_ref, out_pos, in_pos):
    gap = out_pos - in_pos
    near = (gap >= 0) & (gap < FILTER_LEN) & (in_pos >= doc_start(lens_ref, out_pos))
    return near.astype(F32).astype(BF16)


def window_positions(inner, span):
    base = (lax.axis_index("seq") // inner) * span
    shape = (LANES, 2 * LANES)
    return (
        base + lax.broadcasted_iota(jnp.int32, shape, 0),
        base + lax.broadcasted_iota(jnp.int32, shape, 1),
    )


def conv_core_kernel(
    rows, inner, ch_count, lens_ref, tap_ref, rev_ref, prior_ref, m0_ref, m1_ref, g0_ref, g1_ref,
    later_ref, *refs,
):
    members = inner * ch_count
    outs = refs[:members]
    conv_ref, down_ref = refs[members:]
    me = member_index(ch_count, inner)
    groups = LANES // GROUP
    blocks = 2
    down, across = window_positions(inner, members * rows)
    back = [reached(lens_ref, down + b * LANES, across + (b - 1) * LANES) for b in range(blocks)]
    front = [reached(lens_ref, across + b * LANES, down + b * LANES) for b in range(blocks)]

    for tile in range(m0_ref.shape[1] // LANES):
        cols = slice(tile * LANES, (tile + 1) * LANES)
        mixed = [r[:, cols] for r in (prior_ref, m0_ref, m1_ref)]
        grad = [r[:, cols] for r in (g0_ref, g1_ref, later_ref)]
        lane_group = lax.broadcasted_iota(jnp.int32, (LANES, LANES), 1) // GROUP
        tap_rows = slice(tile * groups, (tile + 1) * groups)
        taps, rev_taps = tap_ref[tap_rows, :], rev_ref[tap_rows, :]
        back_taps = [circulant(rev_taps[g : g + 1]) for g in range(groups)]
        front_taps = [circulant(taps[g : g + 1]) for g in range(groups)]
        for b in range(blocks):
            window = jnp.concatenate(mixed[b : b + 2], axis=0)
            ahead = jnp.concatenate(grad[b : b + 2], axis=0)
            conv_all = dot(jnp.concatenate([t * back[b] for t in back_taps], axis=0), window, NN)
            down_all = dot(jnp.concatenate([t * front[b] for t in front_taps], axis=0), ahead, NN)
            conv_out = jnp.zeros((LANES, LANES), F32)
            mixed_grad = jnp.zeros((LANES, LANES), F32)
            for g in range(groups):
                mine = lane_group == g
                span = slice(g * LANES, (g + 1) * LANES)
                conv_out = jnp.where(mine, conv_all[span], conv_out)
                mixed_grad = jnp.where(mine, down_all[span], mixed_grad)
            here = slice(b * LANES, (b + 1) * LANES)
            conv_ref[here, cols] = conv_out.astype(BF16)
            down_ref[here, cols] = mixed_grad.astype(BF16)
    for k, out_ref in enumerate(outs):
        at = pl.multiple_of(jnp.bitwise_xor(me, k) * rows, rows)
        out_ref[0:rows, :] = conv_ref[pl.ds(at, rows), :]
        out_ref[rows : 2 * rows, :] = down_ref[pl.ds(at, rows), :]


def conv_core(lens, taps, rev_taps, arrays, rows, inner, ch_count):
    members = inner * ch_count
    width = arrays[0].shape[1]
    vmem = pl.BlockSpec(memory_space=pltpu.VMEM)
    return pl.pallas_call(
        functools.partial(conv_core_kernel, rows, inner, ch_count),
        in_specs=[pl.BlockSpec(memory_space=pltpu.SMEM)] + [vmem] * 8,
        out_specs=[vmem] * members,
        out_shape=[jax.ShapeDtypeStruct((2 * rows, width), BF16)] * members,
        scratch_shapes=[pltpu.VMEM((2 * LANES, width), BF16)] * 2,
        cost_estimate=cost(2000 * LANES * LANES * width, 24 * LANES * width),
        compiler_params=pltpu.CompilerParams(vmem_limit_bytes=40 * 1024 * 1024),
        name="conv_core",
    )(lens, taps, rev_taps, *arrays)


def conv_filter_kernel(
    rows, inner, ch_count, lens_ref, prior_ref, m0_ref, m1_ref, g0_ref, g1_ref, filt_ref
):
    groups = LANES // GROUP
    blocks = 2
    down, across = window_positions(inner, inner * ch_count * rows)
    back = [
        reached(lens_ref, down + b * LANES, across + (b - 1) * LANES).astype(F32)
        for b in range(blocks)
    ]
    for tile in range(m0_ref.shape[1] // LANES):
        cols = slice(tile * LANES, (tile + 1) * LANES)
        mixed = [r[:, cols] for r in (prior_ref, m0_ref, m1_ref)]
        grad = [r[:, cols] for r in (g0_ref, g1_ref)]
        lane_group = lax.broadcasted_iota(jnp.int32, (LANES, LANES), 1) // GROUP
        sums = []
        for g in range(groups):
            mine = (lane_group == g).astype(F32).astype(BF16)
            outer = jnp.zeros((LANES, LANES), F32)
            for b in range(blocks):
                window = jnp.concatenate(mixed[b : b + 2], axis=0)
                full = dot(grad[b] * mine, window, NT) * back[b]
                outer = outer + full[:, 0:LANES] + full[:, LANES:]
            sums.append(unskewed(outer))
        filt_ref[tile * groups : (tile + 1) * groups, :] = jnp.concatenate(sums, axis=0)


def conv_filter_grad(lens, arrays, rows, inner, ch_count):
    width = arrays[0].shape[1]
    vmem = pl.BlockSpec(memory_space=pltpu.VMEM)
    return pl.pallas_call(
        functools.partial(conv_filter_kernel, rows, inner, ch_count),
        in_specs=[pl.BlockSpec(memory_space=pltpu.SMEM)] + [vmem] * 5,
        out_specs=vmem,
        out_shape=jax.ShapeDtypeStruct((width // GROUP, FILTER_LEN), F32),
        cost_estimate=cost(32 * LANES * LANES * width, 10 * LANES * width),
        compiler_params=pltpu.CompilerParams(vmem_limit_bytes=40 * 1024 * 1024),
        name="conv_filter_grad",
    )(lens, *arrays)


def conv_unpack_kernel(inner, ch_count, each, ck_ref, cv_ref, cg_ref, *refs):
    members = inner * ch_count
    pieces, (gq_ref, gk_ref, gv_ref) = refs[:members], refs[members:]
    rows, width = pieces[0].shape[0] // 2, pieces[0].shape[1]
    for part in range(each):
        piece = chunk_piece(pl.program_id(0) * each + part, ch_count, inner)
        cols = slice(part * width, (part + 1) * width)
        for k, x_ref in enumerate(pieces):

            @pl.when(piece == k)
            def _():
                conv_out = x_ref[0:rows, :].astype(F32)
                mixed_grad = x_ref[rows : 2 * rows, :].astype(F32)
                gq_ref[:, cols] = (cg_ref[:, cols].astype(F32) * conv_out).astype(BF16)
                gk_ref[:, cols] = (mixed_grad * cv_ref[:, cols].astype(F32)).astype(BF16)
                gv_ref[:, cols] = (mixed_grad * ck_ref[:, cols].astype(F32)).astype(BF16)


def conv_unpack(pieces, ck, cv, cg, inner, ch_count):
    rows, channels = ck.shape
    members = inner * ch_count
    each = EACH
    width = each * channels // members
    spec = pl.BlockSpec((rows, width), lambda k: (0, k))
    shape = jax.ShapeDtypeStruct((rows, channels), BF16)
    return pl.pallas_call(
        functools.partial(conv_unpack_kernel, inner, ch_count, each),
        grid=(members // each,),
        in_specs=[spec] * 3 + [pl.BlockSpec(pieces[0].shape, lambda k: (0, 0))] * members,
        out_specs=[spec] * 3,
        out_shape=[shape] * 3,
        compiler_params=params(),
        cost_estimate=cost(6 * rows * channels, 16 * rows * channels),
        name="conv_unpack",
    )(ck, cv, cg, *pieces)


def doc_index(doc_lengths, positions):
    doc_ends = jnp.cumsum(doc_lengths)
    return jnp.sum((doc_ends[None, :] <= positions[:, None]).astype(jnp.int32), axis=1)


def split_rows(advance, carried, pieces):
    def one_block(block_index, current):
        sub_parts = tuple(
            lax.dynamic_slice_in_dim(part, block_index * 512, 512, 0) for part in pieces
        )
        return advance(current, sub_parts, block_index * 512)

    return lax.fori_loop(0, pieces[0].shape[0] // 512, one_block, carried)


def attn_gathered(attn_query, attn_key, attn_value, attn_output, attn_grad_out, doc_lengths):
    query_rows, key_rows, value_rows, output_rows, grad_rows = (
        lax.all_to_all(a, "ch", split_axis=1, concat_axis=0, tiled=True)
        for a in (attn_query, attn_key, attn_value, attn_output, attn_grad_out)
    )
    tok_rows = query_rows.shape[0]
    head_count = query_rows.shape[1] // HEAD_DIM
    scale_factor = 1.0 / math.sqrt(HEAD_DIM)
    local_pos = lax.axis_index("seq") * tok_rows + jnp.arange(tok_rows, dtype=jnp.int32)
    local_doc = doc_index(doc_lengths, local_pos)
    query_heads, key_heads, value_heads, output_heads, grad_heads = (
        a.reshape(tok_rows, head_count, HEAD_DIM)
        for a in (query_rows, key_rows, value_rows, output_rows, grad_rows)
    )
    delta_rows = jnp.sum(grad_heads.astype(F32) * output_heads.astype(F32), axis=2)
    delta_heads = delta_rows.T

    def key_step(carried, pieces, key_start):
        key_part, value_part = pieces
        key_pos = key_start + jnp.arange(key_part.shape[0], dtype=jnp.int32)
        key_doc = doc_index(doc_lengths, key_pos)
        visible = (key_doc[None, :] == local_doc[:, None]) & (key_pos[None, :] <= local_pos[:, None])
        running_max, running_sum, running_grad = carried
        scores = (
            jnp.einsum("thd,rhd->htr", query_heads, key_part, preferred_element_type=F32)
            * scale_factor
        )
        new_max = jnp.maximum(
            running_max, jnp.max(jnp.where(visible[None], scores, NEG_FILL), axis=2)
        )
        weights = jnp.where(visible[None], jnp.exp(scores - new_max[:, :, None]), 0.0)
        rescale = jnp.exp(running_max - new_max)
        grad_probs = jnp.einsum(
            "thd,rhd->htr", grad_heads, value_part, preferred_element_type=F32
        )
        weighted = weights * (grad_probs - delta_heads[:, :, None])
        update = jnp.einsum(
            "htr,rhd->htd", weighted, key_part.astype(F32), precision=lax.Precision.HIGHEST
        )
        return (
            new_max,
            running_sum * rescale + jnp.sum(weights, axis=2),
            running_grad * rescale[:, :, None] + update,
        )

    start_state = (
        jnp.full((head_count, tok_rows), NEG_FILL, F32),
        jnp.zeros((head_count, tok_rows), F32),
        jnp.zeros((head_count, tok_rows, HEAD_DIM), F32),
    )
    final_max, final_sum, final_grad = split_rows(
        key_step,
        start_state,
        (
            lax.all_gather(key_heads, "seq", axis=0, tiled=True),
            lax.all_gather(value_heads, "seq", axis=0, tiled=True),
        ),
    )
    lse_rows = (final_max + jnp.log(final_sum)).T
    grad_query = (final_grad * (scale_factor / final_sum)[:, :, None]).transpose(1, 0, 2)
    lse_whole = lax.all_gather(lse_rows, "seq", axis=0, tiled=True)
    delta_whole = lax.all_gather(delta_rows, "seq", axis=0, tiled=True)

    def query_step(carried, pieces, query_start):
        query_part, grad_part = pieces
        part_rows = query_part.shape[0]
        lse_part = lax.dynamic_slice_in_dim(lse_whole, query_start, part_rows, 0)
        delta_part = lax.dynamic_slice_in_dim(delta_whole, query_start, part_rows, 0)
        query_pos = query_start + jnp.arange(part_rows, dtype=jnp.int32)
        query_doc = doc_index(doc_lengths, query_pos)
        visible = (query_doc[:, None] == local_doc[None, :]) & (
            local_pos[None, :] <= query_pos[:, None]
        )
        key_grad, value_grad = carried
        scores = (
            jnp.einsum("rhd,thd->hrt", query_part, key_heads, preferred_element_type=F32)
            * scale_factor
        )
        probs = jnp.where(visible[None], jnp.exp(scores - lse_part.T[:, :, None]), 0.0)
        value_grad = value_grad + jnp.einsum(
            "hrt,rhd->thd", probs, grad_part.astype(F32), precision=lax.Precision.HIGHEST
        )
        grad_probs = jnp.einsum(
            "rhd,thd->hrt", grad_part, value_heads, preferred_element_type=F32
        )
        grad_scores = probs * (grad_probs - delta_part.T[:, :, None])
        key_grad = key_grad + scale_factor * jnp.einsum(
            "hrt,rhd->thd", grad_scores, query_part.astype(F32), precision=lax.Precision.HIGHEST
        )
        return (key_grad, value_grad)

    zero = jnp.zeros((tok_rows, head_count, HEAD_DIM), F32)
    key_grad, value_grad = split_rows(
        query_step,
        (zero, zero),
        (
            lax.all_gather(query_heads, "seq", axis=0, tiled=True),
            lax.all_gather(grad_heads, "seq", axis=0, tiled=True),
        ),
    )
    return tuple(
        lax.all_to_all(
            a.reshape(tok_rows, head_count * HEAD_DIM).astype(BF16),
            "ch",
            split_axis=0,
            concat_axis=1,
            tiled=True,
        )
        for a in (grad_query, key_grad, value_grad)
    )


def shifted(block, distance, count):
    route = [(i, i + distance) for i in range(count) if 0 <= i + distance < count]
    return lax.ppermute(block, DEVICES, route)


def exchanged(block, distance, count):
    return lax.ppermute(block, DEVICES, [(i, i ^ distance) for i in range(count)])


def body(
    attn_query, attn_key, attn_value, attn_output, attn_grad_out,
    conv_query, conv_key, conv_value, conv_grad_out, conv_filter, doc_lengths,
):
    seq_count, ch_count = lax.axis_size("seq"), lax.axis_size("ch")
    count = seq_count * ch_count
    rows, channels = conv_query.shape
    inner = 2
    members = inner * ch_count
    outer = seq_count // inner
    heads = attn_query.shape[1] // HEAD_DIM
    head_each = heads == count

    reach = BAND_REACH if rows * count == 1024 else rows * count

    if head_each:
        attn_packed = attn_pack(attn_query, attn_key, attn_value, attn_output, attn_grad_out)
        attn_in = lax.all_to_all(attn_packed, DEVICES, split_axis=0, concat_axis=0, tiled=True)

    packed = conv_pack(conv_query, conv_key, conv_value, conv_grad_out, inner, ch_count)
    packed = list(packed)
    pieces = [packed[0], exchanged(packed[1], 1, count)]
    packed[-1], pieces[1] = lax.optimization_barrier((packed[-1], pieces[1]))
    pieces += [exchanged(packed[k], k, count) for k in range(2, members)]
    group_count = channels // members // GROUP
    y = lax.rem(lax.axis_index("seq"), inner)
    taps = lax.dynamic_slice_in_dim(conv_filter, y * group_count, group_count, 0).astype(F32)
    rev_taps = jnp.roll(taps[:, ::-1], 1, axis=1)
    taps, rev_taps, *pieces = lax.optimization_barrier((taps, rev_taps, *pieces))
    mixed_lo, mixed_hi, grad_lo, grad_hi = conv_join(pieces, rows, inner, ch_count)
    if head_each:
        attn_in, mixed_hi, grad_lo = lax.optimization_barrier((attn_in, mixed_hi, grad_lo))
    prior, later = shifted(mixed_hi, members, count), shifted(grad_lo, -members, count)
    if head_each:
        attn_back = attn_head(doc_lengths, attn_in, rows, reach)
        attn_back, taps, rev_taps = lax.optimization_barrier((attn_back, taps, rev_taps))
        attn_res = lax.all_to_all(attn_back, DEVICES, split_axis=0, concat_axis=0, tiled=True)
    own = (prior, mixed_lo, mixed_hi, grad_lo, grad_hi, later)
    filter_part = conv_filter_grad(doc_lengths, own[:5], rows, inner, ch_count)
    other = exchanged(filter_part, members, count)
    taps, filter_part = lax.optimization_barrier((taps, filter_part))
    conv_back = conv_core(doc_lengths, taps, rev_taps, own, rows, inner, ch_count)
    conv_back = list(conv_back)
    conv_res = [conv_back[0], exchanged(conv_back[1], 1, count)]
    conv_back[-1], conv_res[1] = lax.optimization_barrier((conv_back[-1], conv_res[1]))
    conv_res += [exchanged(conv_back[k], k, count) for k in range(2, members)]
    filter_part, other, conv_res[1:4] = lax.optimization_barrier(
        (filter_part, other, conv_res[1:4])
    )
    filter_part = filter_part + other
    distance = 2 * members
    while distance < count:
        other = exchanged(filter_part, distance, count)
        conv_res, other = lax.optimization_barrier((conv_res, other))
        filter_part = filter_part + other
        distance *= 2
    filter_part = jnp.roll(filter_part[:, ::-1], 1, axis=1)
    other = exchanged(filter_part, ch_count, count)
    grad_conv = conv_unpack(conv_res, conv_key, conv_value, conv_grad_out, inner, ch_count)
    other, *grad_conv = lax.optimization_barrier((other, *grad_conv))
    if head_each:
        *grad_attn, grad_filter = attn_unpack(attn_res, filter_part, other, rows, inner)
    else:
        grad_attn = attn_gathered(
            attn_query, attn_key, attn_value, attn_output, attn_grad_out, doc_lengths
        )
        grad_filter = jnp.where(
            y == 0,
            jnp.concatenate([filter_part, other], axis=0),
            jnp.concatenate([other, filter_part], axis=0),
        )
    return (*grad_attn, *grad_conv, grad_filter)


def solution(mesh):
    rows = P(("seq", "ch"), None)
    return jax.shard_map(
        body,
        mesh=mesh,
        in_specs=(rows,) * 9 + (P("ch", None), P()),
        out_specs=(rows,) * 6 + (P("ch", None),),
        check_vma=False,
    )
```
